256 devices in a mesh: section: 8 (over z_lo, x), dp: 32 (over z_hi, y, core).
Axes of the slice: x: 4, y: 4, z: 8 (z_hi: 4, z_lo: 2; z = z_hi * 2 + z_lo), core: 2. Of those that a mesh axis runs over, the one named last changes fastest.
Arguments:
- inputs: bfloat16 [4, 1024, 4096], P(None, 'dp'), may hold values from -6 to 6
- cotangent: bfloat16 [4, 1024, 4096], P(None, 'dp'), may hold values from -0.09375 to 0.09375
- up_blocks: bfloat16 [8, 128, 128, 128], P('section', 'dp'), may hold values from -0.5 to 0.5
- up_index: int32 [8, 128, 2], P('section'), may hold values from 0 to 127, as said below
- up_left: bfloat16 [8, 4096, 16], P('section', 'dp'), may hold values from -0.09375 to 0.09375
- up_right: bfloat16 [8, 16384, 16], P('section', 'dp'), may hold values from -1.5 to 1.5
- down_blocks: bfloat16 [8, 128, 128, 128], P('section', 'dp'), may hold values from -0.25 to 0.25
- down_index: int32 [8, 128, 2], P('section'), may hold values from 0 to 127, as said below
- down_left: bfloat16 [8, 16384, 16], P('section', 'dp'), may hold values from -0.046875 to 0.046875
- down_right: bfloat16 [8, 4096, 16], P('section', 'dp'), may hold values from -1.5 to 1.5
Outputs:
- section_outputs: bfloat16 [8, 4, 1024, 4096], P('section', None, 'dp')
- up_grad: float32 [8, 128, 128, 128], P('section', 'dp')
- up_left_grad: float32 [8, 4096, 16], P('section', 'dp')
- up_right_grad: float32 [8, 16384, 16], P('section', 'dp')
- down_grad: float32 [8, 128, 128, 128], P('section', 'dp')
- down_left_grad: float32 [8, 16384, 16], P('section', 'dp')
- down_right_grad: float32 [8, 4096, 16], P('section', 'dp')
The draws below stay inside these ranges and needn't reach their ends.
Inputs may be any that keep to these rules, and one draw needn't show every extreme that they name: `up_index`: column 0 is a block of model features (below 32), column 1 a block of hidden units; rows 4 * p to 4 * p + 3 hold model block p, and no pair repeats within a section. `down_index`: column 0 is a block of hidden units, column 1 a block of model features (below 32); rows 4 * p to 4 * p + 3 hold model block p, and no pair repeats within a section.
All inputs are finite; a program needn't handle non-finite values.
Results may differ from the reference program's by a relative error of at most 0.04.
Values may be sent and summed in bfloat16 or wider, within the bound.
No kernel may reach another device: no remote copies, remote signals or barrier semaphores. Data moves between devices by JAX's collectives and lax.ppermute only.
A program may use at most 128 MiB of HBM per device.

```python
import math
from functools import partial
import jax
import jax.numpy as jnp
from jax import lax

D = 4096
FF = 16384
BLK = 128
PER_ROW = 4
RANK = 16
ROWS = 32
MICRO = 4
SECTIONS = 8
TOKENS = 1024
NB = 128
N_DP = 32


def block_pairs(key, near_count, far_count):
    stretch = far_count // near_count
    masks = jnp.concatenate([jnp.zeros((1,), jnp.int32), jnp.left_shift(jnp.int32(1), jnp.arange(PER_ROW - 1, dtype=jnp.int32))])
    bases = jnp.arange(near_count, dtype=jnp.int32) * stretch
    slots = jnp.bitwise_xor(bases[:, None], masks[None, :]).reshape(-1)
    section_keys = jax.random.split(key, SECTIONS)
    relabel = jax.vmap(lambda one: jax.random.permutation(one, far_count).astype(jnp.int32))(section_keys)
    far_blocks = relabel[:, slots]
    near_blocks = jnp.broadcast_to(jnp.repeat(jnp.arange(near_count, dtype=jnp.int32), PER_ROW)[None, :], far_blocks.shape)
    return (near_blocks, far_blocks)


def draw_up_index(key, part):
    key = jax.random.fold_in(key, 11)
    near_blocks, far_blocks = block_pairs(key, D // BLK, FF // BLK)
    return jnp.stack([near_blocks, far_blocks], axis=-1).astype(jnp.int32)


def draw_down_index(key, part):
    key = jax.random.fold_in(key, 23)
    near_blocks, far_blocks = block_pairs(key, D // BLK, FF // BLK)
    return jnp.stack([far_blocks, near_blocks], axis=-1).astype(jnp.int32)


def steps_of(stream_key, dims, shards, low, top_value):
    loudness, own = 1.0, jax.random.fold_in(stream_key, 6)
    for position, shards_of in shards:
        heights = jnp.exp(jax.random.uniform(jax.random.fold_in(own, position), (shards_of,), jnp.float32, low / len(shards), top_value / len(shards)))
        loudness = loudness * jnp.repeat(heights, dims[position] // shards_of).reshape([-1 if axis == position else 1 for axis in range(len(dims))])
    return loudness


def centred(own_key, extent, scale, limit, cuts=(), kind=jnp.bfloat16):
    result = scale * jax.random.normal(own_key, extent, jnp.float32)
    if cuts:
        result = result * steps_of(own_key, extent, cuts, -0.22, 0.18)
    return jnp.clip(result, -limit, limit).astype(kind)


def setup_inputs(seed: int = 0) -> dict:
    seeds = jax.random.split(jax.random.key(seed), 11)
    inputs = centred(seeds[0], (MICRO, TOKENS, D), 1.0, 6.0, ((1, 32),))
    cotangent = centred(seeds[1], (MICRO, TOKENS, D), 0.015625, 0.09375, ((1, 32),))
    up_blocks = centred(seeds[2], (SECTIONS, NB, BLK, BLK), BLK ** -0.5, 0.5, ((0, 8), (1, 32)))
    up_index = draw_up_index(jax.random.fold_in(seeds[10], 71), 0)
    up_left = centred(seeds[4], (SECTIONS, D, RANK), D ** -0.5, 0.09375, ((0, 8), (1, 32)))
    up_right = centred(seeds[5], (SECTIONS, FF, RANK), RANK ** -0.5, 1.5, ((0, 8), (1, 32)))
    down_blocks = centred(seeds[6], (SECTIONS, NB, BLK, BLK), (BLK * PER_ROW) ** -0.5, 0.25, ((0, 8), (1, 32)))
    down_index = draw_down_index(jax.random.fold_in(seeds[10], 71), 0)
    down_left = centred(seeds[8], (SECTIONS, FF, RANK), FF ** -0.5, 0.046875, ((0, 8), (1, 32)))
    down_right = centred(seeds[9], (SECTIONS, D, RANK), RANK ** -0.5, 1.5, ((0, 8), (1, 32)))
    return {"inputs": inputs, "cotangent": cotangent, "up_blocks": up_blocks, "up_index": up_index, "up_left": up_left, "up_right": up_right, "down_blocks": down_blocks, "down_index": down_index, "down_left": down_left, "down_right": down_right}


NORM_EPS = 1e-05
GELU_CUBIC = 0.044715
GELU_ROOT = math.sqrt(2.0 / math.pi)

def gelu_parts(values):
    inner = GELU_ROOT * (values + GELU_CUBIC * values * values * values)
    bend = jnp.tanh(inner)
    output = 0.5 * values * (1.0 + bend)
    slopes = 0.5 * (1.0 + bend) + 0.5 * values * (1.0 - bend * bend) * GELU_ROOT * (1.0 + 3.0 * GELU_CUBIC * values * values)
    return (output, slopes)

def spread(products, target, count):
    merged = jnp.zeros((products.shape[0], count, products.shape[2]), products.dtype).at[:, target].add(products)
    return merged.reshape(products.shape[0], count * products.shape[2])

def block_product(values, tiles, source, target, count):
    tile_size = tiles.shape[-1]
    pieces = values.reshape(values.shape[0], -1, tile_size)[:, source].astype(jnp.float32)
    products = jnp.einsum('tnb,nbc->tnc', pieces, tiles.astype(jnp.float32), precision=lax.Precision.HIGHEST)
    return spread(products, target, count)

def block_transpose(grads, tiles, source, target, count):
    tile_size = tiles.shape[-1]
    pieces = grads.reshape(grads.shape[0], -1, tile_size)[:, target].astype(jnp.float32)
    products = jnp.einsum('tnc,nbc->tnb', pieces, tiles.astype(jnp.float32), precision=lax.Precision.HIGHEST)
    return spread(products, source, count)

def block_grad(values, grads, source, target, tile_size):
    left_pieces = values.reshape(values.shape[0], -1, tile_size)[:, source].astype(jnp.float32)
    right_pieces = grads.reshape(grads.shape[0], -1, tile_size)[:, target].astype(jnp.float32)
    return jnp.einsum('tnb,tnc->nbc', left_pieces, right_pieces, precision=lax.Precision.HIGHEST)

def outer_sum(left_rows, right_rows):
    return jnp.dot(left_rows.T, right_rows, preferred_element_type=jnp.float32)

def hidden_parts(values, weights):
    up_tiles, up_pairs, up_left, up_right, down_tiles, down_pairs, down_left, down_right = weights
    hidden_blocks = up_right.shape[0] // up_tiles.shape[-1]
    widened = values.astype(jnp.float32)
    scaling = lax.rsqrt(lax.optimization_barrier(jnp.mean(widened * widened, axis=-1, keepdims=True)) + NORM_EPS)
    normed = (widened * scaling).astype(jnp.bfloat16)
    up_latent = jnp.dot(normed, up_left, preferred_element_type=jnp.float32).astype(jnp.bfloat16)
    lowrank_up = jnp.dot(up_latent, up_right.T, preferred_element_type=jnp.float32)
    pre_act = block_product(normed, up_tiles, up_pairs[:, 0], up_pairs[:, 1], hidden_blocks) + lowrank_up
    output, slopes = gelu_parts(pre_act)
    activation = output.astype(jnp.bfloat16)
    down_latent = jnp.dot(activation, down_left, preferred_element_type=jnp.float32).astype(jnp.bfloat16)
    return (widened, scaling, normed, up_latent, slopes, activation, down_latent)

def layer_forward(values, weights):
    widened, scaling, normed, up_latent, slopes, activation, down_latent = hidden_parts(values, weights)
    down_tiles, down_pairs, down_right = (weights[4], weights[5], weights[7])
    model_blocks = values.shape[1] // down_tiles.shape[-1]
    summed = widened + block_product(activation, down_tiles, down_pairs[:, 0], down_pairs[:, 1], model_blocks)
    summed = summed + jnp.dot(down_latent, down_right.T, preferred_element_type=jnp.float32)
    return summed.astype(jnp.bfloat16)

def layer_backward(values, grad_out, weights):
    up_tiles, up_pairs, up_left, up_right, down_tiles, down_pairs, down_left, down_right = weights
    widened, scaling, normed, up_latent, slopes, activation, down_latent = hidden_parts(values, weights)
    tile_size = up_tiles.shape[-1]
    hidden_blocks = up_right.shape[0] // tile_size
    model_blocks = values.shape[1] // tile_size
    grad_down_latent = jnp.dot(grad_out, down_right, preferred_element_type=jnp.float32).astype(jnp.bfloat16)
    grad_act = block_transpose(grad_out, down_tiles, down_pairs[:, 0], down_pairs[:, 1], hidden_blocks)
    grad_act = grad_act + jnp.dot(grad_down_latent, down_left.T, preferred_element_type=jnp.float32)
    grad_pre = (grad_act * slopes).astype(jnp.bfloat16)
    grad_up_latent = jnp.dot(grad_pre, up_right, preferred_element_type=jnp.float32).astype(jnp.bfloat16)
    grad_norm = block_transpose(grad_pre, up_tiles, up_pairs[:, 0], up_pairs[:, 1], model_blocks)
    grad_norm = grad_norm + jnp.dot(grad_up_latent, up_left.T, preferred_element_type=jnp.float32)
    unit = widened * scaling
    grad_in = grad_out.astype(jnp.float32) + scaling * (grad_norm - unit * lax.optimization_barrier(jnp.mean(grad_norm * unit, axis=-1, keepdims=True)))
    stash = (normed, grad_pre, up_latent, grad_up_latent, activation, grad_out, down_latent, grad_down_latent)
    return (grad_in.astype(jnp.bfloat16), stash)

def pair_backward(pair, weights):
    return layer_backward(pair[0], pair[1], weights)

def group_terms(group, weights):
    normed, grad_pre, up_latent, grad_up_latent, activation, grad_out, down_latent, grad_down_latent = group
    up_pairs, down_pairs = (weights[1], weights[5])
    tile_size = weights[0].shape[-1]
    return (block_grad(normed, grad_pre, up_pairs[:, 0], up_pairs[:, 1], tile_size), outer_sum(normed, grad_up_latent), outer_sum(grad_pre, up_latent), block_grad(activation, grad_out, down_pairs[:, 0], down_pairs[:, 1], tile_size), outer_sum(activation, grad_down_latent), outer_sum(grad_out, down_latent))

def regroup(array):
    shaped = array.reshape(MICRO, N_DP, ROWS, array.shape[-1])
    return jnp.moveaxis(shaped, 1, 0).reshape(N_DP, MICRO * ROWS, array.shape[-1])

def summed_grads(stash, weights):
    grouped = tuple((regroup(item) for item in stash))

    def add_group(totals, group):
        terms = group_terms(group, weights)
        rounded = tuple((lax.optimization_barrier(term.astype(jnp.bfloat16)).astype(jnp.float32) for term in terms))
        return (tuple((total + term for total, term in zip(totals, rounded))), None)
    shapes = (weights[0].shape, weights[2].shape, weights[3].shape, weights[4].shape, weights[6].shape, weights[7].shape)
    zeros = tuple((jnp.zeros(shape, jnp.float32) for shape in shapes))
    totals, unused = lax.scan(add_group, zeros, grouped)
    return totals

def reference(inputs, cotangent, up_blocks, up_index, up_left, up_right, down_blocks, down_index, down_left, down_right):
    every = (up_blocks, up_index, up_left, up_right, down_blocks, down_index, down_left, down_right)
    saved = []
    produced = []
    current = inputs
    for section in range(SECTIONS):
        weights = tuple((item[section] for item in every))
        saved.append(current)
        current = lax.map(partial(layer_forward, weights=weights), current)
        produced.append(current)
    results = [None] * SECTIONS
    incoming = cotangent
    for section in range(SECTIONS - 1, -1, -1):
        weights = tuple((item[section] for item in every))
        grad_in, stash = lax.map(partial(pair_backward, weights=weights), (saved[section], incoming))
        results[section] = summed_grads(stash, weights)
        incoming = grad_in
    stacked = [jnp.stack([results[section][member] for section in range(SECTIONS)]) for member in range(6)]
    return (jnp.stack(produced), stacked[0], stacked[1], stacked[2], stacked[3], stacked[4], stacked[5])
```

```python
import math
from functools import partial

import jax
import jax.numpy as jnp
from jax import lax
from jax.experimental import pallas as pl
from jax.experimental.pallas import tpu as pltpu
from jax.sharding import Mesh
from jax.sharding import PartitionSpec as P

NORM_EPS = 1e-05
GELU_CUBIC = 0.044715
GELU_ROOT = math.sqrt(2.0 / math.pi)

TILE = 128
PER_ROW = 4
RANK = 16
UP = 0
DOWN = PER_ROW * TILE
LOW = 2 * PER_ROW * TILE
UP_LEFT = LOW
UP_RIGHT = UP_LEFT + RANK
DOWN_LEFT = UP_RIGHT + PER_ROW * RANK
DOWN_RIGHT = DOWN_LEFT + PER_ROW * RANK
PACKED = DOWN_RIGHT + RANK
WEIGHT_CHUNKS = 8
VMEM_LIMIT = 48 * 1024 * 1024
F32 = jnp.float32
BF16 = jnp.bfloat16


def mm(left, right):
    return lax.dot_general(left, right, (((1,), (0,)), ((), ())), preferred_element_type=F32)


def mm_nt(left, right):
    return lax.dot_general(left, right, (((1,), (1,)), ((), ())), preferred_element_type=F32)


def mm_tn(left, right):
    return lax.dot_general(left, right, (((0,), (0,)), ((), ())), preferred_element_type=F32)


def lanes(pieces):
    return jnp.concatenate(pieces, axis=1)


def low_rows(w, base, index):
    return lanes([w[index, base + RANK * i : base + RANK * (i + 1), :] for i in range(PER_ROW)])


def weight_copies(w_hbm, w, sem, first, second):
    blocks = w.shape[0]
    step = blocks // WEIGHT_CHUNKS
    copies = [
        pltpu.make_async_copy(w_hbm.at[:, LOW:PACKED, :], w.at[:, LOW:PACKED, :], sem.at[0])
    ]
    for number, base in enumerate((first, second)):
        for chunk in range(WEIGHT_CHUNKS):
            rows = pl.ds(chunk * step, step)
            cols = pl.ds(base, PER_ROW * TILE)
            copies.append(
                pltpu.make_async_copy(
                    w_hbm.at[rows, cols, :],
                    w.at[rows, cols, :],
                    sem.at[1 + number * WEIGHT_CHUNKS + chunk],
                )
            )
    return copies


def normalised(x_ref):
    xf = x_ref[...].astype(F32)
    scaling = lax.rsqrt(jnp.mean(xf * xf, axis=-1, keepdims=True) + NORM_EPS)
    return xf, scaling


def forward_kernel(
    info, upq, dnq, inputs, incoming, w_hbm, xs_in, outs_in, act_in, slope_in, lat_in,
    y_hbm, xs, outs, act, slope, lat,
    w, x, pre, av, sv, y, latv, sem, in_sem, out_sem,
):
    live, slot, first = info[0], info[1], info[2]
    blocks = w.shape[0]
    hidden = pre.shape[0]
    step = blocks // WEIGHT_CHUNKS

    @pl.when(live == 1)
    def _():
        @pl.when(first == 1)
        def _():
            pltpu.make_async_copy(inputs.at[slot], x, in_sem).start()

        @pl.when(first == 0)
        def _():
            pltpu.make_async_copy(incoming, x, in_sem).start()

        copies = weight_copies(w_hbm, w, sem, UP, DOWN)
        for copy in copies:
            copy.start()
        pltpu.make_async_copy(incoming, x, in_sem).wait()
        keep_x = pltpu.make_async_copy(x, xs.at[slot], out_sem.at[0])
        keep_x.start()
        xf, scaling = normalised(x)
        normed = (xf * scaling).astype(BF16)
        copies[0].wait()
        up_latent = jnp.zeros((x.shape[0], RANK), F32)
        for j in range(0, blocks, 2):
            up_latent += mm_nt(
                normed[:, j * TILE : (j + 2) * TILE],
                lanes([w[j + i, UP_LEFT : UP_LEFT + RANK, :] for i in range(2)]),
            )
        up_latent = up_latent.astype(BF16)
        latv[0, :, 0:RANK] = up_latent
        for p in range(blocks):
            low = mm(up_latent, low_rows(w, UP_RIGHT, p))
            for i in range(PER_ROW):
                pre[PER_ROW * p + i] = low[:, i * TILE : (i + 1) * TILE]
        for p in range(blocks):
            if p % step == 0:
                copies[1 + p // step].wait()
            piece = lanes([w[p, UP + i * TILE : UP + (i + 1) * TILE, :] for i in range(PER_ROW)])
            product = mm(normed[:, p * TILE : (p + 1) * TILE], piece)
            where = [upq[PER_ROW * p + i] for i in range(PER_ROW)]
            sums = [pre[q] + product[:, i * TILE : (i + 1) * TILE] for i, q in enumerate(where)]
            for q, value in zip(where, sums):
                pre[q] = value

        def gelu(q, carry):
            u = pre[q]
            square = u * u
            bend = jnp.tanh(GELU_ROOT * (u * (1.0 + GELU_CUBIC * square)))
            half = 0.5 + 0.5 * bend
            av[q] = (u * half).astype(BF16)
            slopes = half + 0.5 * u * (1.0 - bend * bend) * (
                GELU_ROOT * (1.0 + 3.0 * GELU_CUBIC * square)
            )
            sv[q] = slopes.astype(BF16)
            return carry

        lax.fori_loop(0, hidden, gelu, 0, unroll=8)
        keep_act = pltpu.make_async_copy(av, act.at[slot], out_sem.at[1])
        keep_slope = pltpu.make_async_copy(sv, slope.at[slot], out_sem.at[2])
        keep_act.start()
        keep_slope.start()
        down_latent = jnp.zeros((x.shape[0], RANK), F32)
        for p in range(blocks):
            down_latent += mm_nt(
                lanes([av[PER_ROW * p + i] for i in range(PER_ROW)]), low_rows(w, DOWN_LEFT, p)
            )
        down_latent = down_latent.astype(BF16)
        latv[1, :, 0:RANK] = down_latent
        keep_lat = pltpu.make_async_copy(latv, lat.at[slot], out_sem.at[3])
        keep_lat.start()
        for p in range(blocks):
            if p % step == 0:
                copies[1 + WEIGHT_CHUNKS + p // step].wait()
            left = lanes([av[dnq[PER_ROW * p + i]] for i in range(PER_ROW)])
            product = mm(left, w[p, DOWN : DOWN + PER_ROW * TILE, :])
            product += mm(down_latent, w[p, DOWN_RIGHT : DOWN_RIGHT + RANK, :])
            cols = slice(p * TILE, (p + 1) * TILE)
            y[:, cols] = (x[:, cols].astype(F32) + product).astype(BF16)
        send = pltpu.make_async_copy(y, y_hbm, out_sem.at[4])
        keep_y = pltpu.make_async_copy(y, outs.at[slot], out_sem.at[5])
        send.start()
        keep_y.start()
        for copy in (keep_x, keep_act, keep_slope, keep_lat, send, keep_y):
            copy.wait()


def backward_kernel(
    info, upq, dnq, cotangent, incoming, w_hbm, xs, slope, gs_in, gp_in, lat_in,
    y_hbm, gs, gp, lat,
    w, x, g, ga, sv, gpv, y, norm, latv, sem, in_sem, out_sem,
):
    live, slot, first = info[0], info[1], info[2]
    blocks = w.shape[0]
    hidden = ga.shape[0]
    step = blocks // WEIGHT_CHUNKS

    @pl.when(live == 1)
    def _():
        @pl.when(first == 1)
        def _():
            pltpu.make_async_copy(cotangent.at[slot], g, in_sem.at[0]).start()

        @pl.when(first == 0)
        def _():
            pltpu.make_async_copy(incoming, g, in_sem.at[0]).start()

        copies = weight_copies(w_hbm, w, sem, DOWN, UP)
        for copy in copies:
            copy.start()
        get_x = pltpu.make_async_copy(xs.at[slot], x, in_sem.at[1])
        get_slope = pltpu.make_async_copy(slope.at[slot], sv, in_sem.at[2])
        get_slope.start()
        get_x.start()
        pltpu.make_async_copy(incoming, g, in_sem.at[0]).wait()
        keep_g = pltpu.make_async_copy(g, gs.at[slot], out_sem.at[0])
        keep_g.start()
        copies[0].wait()
        down = jnp.zeros((g.shape[0], RANK), F32)
        for j in range(0, blocks, 2):
            down += mm_nt(
                g[:, j * TILE : (j + 2) * TILE],
                lanes([w[j + i, DOWN_RIGHT : DOWN_RIGHT + RANK, :] for i in range(2)]),
            )
        down = down.astype(BF16)
        latv[1, :, 0:RANK] = down
        for p in range(blocks):
            low = mm(down, low_rows(w, DOWN_LEFT, p))
            for i in range(PER_ROW):
                ga[PER_ROW * p + i] = low[:, i * TILE : (i + 1) * TILE]
        for p in range(blocks):
            if p % step == 0:
                copies[1 + p // step].wait()
            product = mm_nt(g[:, p * TILE : (p + 1) * TILE], w[p, DOWN : DOWN + PER_ROW * TILE, :])
            where = [dnq[PER_ROW * p + i] for i in range(PER_ROW)]
            sums = [ga[q] + product[:, i * TILE : (i + 1) * TILE] for i, q in enumerate(where)]
            for q, value in zip(where, sums):
                ga[q] = value
        get_slope.wait()

        def slopes(q, carry):
            gpv[q] = (ga[q] * sv[q].astype(F32)).astype(BF16)
            return carry

        lax.fori_loop(0, hidden, slopes, 0, unroll=8)
        keep_gp = pltpu.make_async_copy(gpv, gp.at[slot], out_sem.at[1])
        keep_gp.start()
        up = jnp.zeros((g.shape[0], RANK), F32)
        for p in range(blocks):
            up += mm_nt(
                lanes([gpv[PER_ROW * p + i] for i in range(PER_ROW)]), low_rows(w, UP_RIGHT, p)
            )
        up = up.astype(BF16)
        latv[0, :, 0:RANK] = up
        keep_lat = pltpu.make_async_copy(latv, lat.at[slot], out_sem.at[2])
        keep_lat.start()
        get_x.wait()
        xf, scaling = normalised(x)
        along = jnp.zeros((g.shape[0], TILE), F32)
        for p in range(blocks):
            if p % step == 0:
                copies[1 + WEIGHT_CHUNKS + p // step].wait()
            left = lanes([gpv[upq[PER_ROW * p + i]] for i in range(PER_ROW)])
            piece = lanes([w[p, UP + i * TILE : UP + (i + 1) * TILE, :] for i in range(PER_ROW)])
            product = mm_nt(left, piece)
            product += mm(up, w[p, UP_LEFT : UP_LEFT + RANK, :])
            cols = slice(p * TILE, (p + 1) * TILE)
            norm[:, cols] = product
            along += product * (xf[:, cols] * scaling)
        mean = jnp.sum(along, axis=-1, keepdims=True) * (1.0 / (blocks * TILE))
        y[...] = (
            g[...].astype(F32) + scaling * (norm[...] - (xf * scaling) * mean)
        ).astype(BF16)
        send = pltpu.make_async_copy(y, y_hbm, out_sem.at[3])
        send.start()
        for copy in (keep_g, keep_gp, keep_lat, send):
            copy.wait()


def grads_kernel(upq, dnq, xs, gs, act, gp, flat, blat, out, normed):
    blocks = out.shape[0]
    micro, rows, width = xs.shape
    tokens = micro * rows
    xf, scaling = normalised(xs)
    normed[...] = (xf * scaling).astype(BF16)

    def column(ref, p):
        return ref[:, :, pl.ds(pl.multiple_of(p * TILE, TILE), TILE)].reshape(tokens, TILE)

    def hidden(ref, q):
        return ref[:, pl.ds(q, 1)].reshape(tokens, TILE)

    def latent(ref, kind):
        return ref[:, kind, :, 0:RANK].reshape(tokens, RANK)

    up_latent, down_latent = latent(flat, 0), latent(flat, 1)
    grad_up_latent, grad_down_latent = latent(blat, 0), latent(blat, 1)

    def one(p, carry):
        n, g = column(normed, p), column(gs, p)
        ups = [upq[PER_ROW * p + i] for i in range(PER_ROW)]
        downs = [dnq[PER_ROW * p + i] for i in range(PER_ROW)]
        up = mm_tn(n, lanes([hidden(gp, q) for q in ups]))
        for i in range(PER_ROW):
            out[p, UP + i * TILE : UP + (i + 1) * TILE, :] = up[:, i * TILE : (i + 1) * TILE].astype(BF16)
        for i, q in enumerate(downs):
            out[p, DOWN + i * TILE : DOWN + (i + 1) * TILE, :] = mm_tn(hidden(act, q), g).astype(BF16)
        out[p, UP_LEFT : UP_LEFT + RANK, :] = mm_tn(grad_up_latent, n).astype(BF16)
        out[p, DOWN_RIGHT : DOWN_RIGHT + RANK, :] = mm_tn(down_latent, g).astype(BF16)
        for base, rows_of, ref in ((UP_RIGHT, up_latent, gp), (DOWN_LEFT, grad_down_latent, act)):
            low = mm_tn(rows_of, lanes([hidden(ref, PER_ROW * p + i) for i in range(PER_ROW)]))
            for i in range(PER_ROW):
                out[p, base + RANK * i : base + RANK * (i + 1), :] = low[:, i * TILE : (i + 1) * TILE].astype(BF16)
        return carry

    lax.fori_loop(0, blocks, one, 0)


SMEM = pl.BlockSpec(memory_space=pltpu.SMEM)
VMEM = pl.BlockSpec(memory_space=pltpu.VMEM)
HBM = pl.BlockSpec(memory_space=pl.ANY)


def forward_call(info, upq, dnq, inputs, incoming, packed, kept):
    rows, width = incoming.shape
    blocks = packed.shape[0]
    hidden = blocks * PER_ROW
    return pl.pallas_call(
        forward_kernel,
        out_shape=(jax.ShapeDtypeStruct(incoming.shape, BF16),)
        + tuple(jax.ShapeDtypeStruct(item.shape, item.dtype) for item in kept),
        in_specs=[SMEM] * 3 + [HBM] * (3 + len(kept)),
        out_specs=(HBM,) * (1 + len(kept)),
        input_output_aliases={6 + i: 1 + i for i in range(len(kept))},
        scratch_shapes=[
            pltpu.VMEM(packed.shape, BF16),
            pltpu.VMEM((rows, width), BF16),
            pltpu.VMEM((hidden, rows, TILE), F32),
            pltpu.VMEM((hidden, rows, TILE), BF16),
            pltpu.VMEM((hidden, rows, TILE), BF16),
            pltpu.VMEM((rows, width), BF16),
            pltpu.VMEM((2, rows, TILE), BF16),
            pltpu.SemaphoreType.DMA((1 + 2 * WEIGHT_CHUNKS,)),
            pltpu.SemaphoreType.DMA,
            pltpu.SemaphoreType.DMA((6,)),
        ],
        compiler_params=pltpu.CompilerParams(vmem_limit_bytes=VMEM_LIMIT),
        name="layer_forward",
    )(info, upq, dnq, inputs, incoming, packed, *kept)


def backward_call(info, upq, dnq, cotangent, incoming, packed, xs, slope, kept):
    rows, width = incoming.shape
    blocks = packed.shape[0]
    hidden = blocks * PER_ROW
    return pl.pallas_call(
        backward_kernel,
        out_shape=(jax.ShapeDtypeStruct(incoming.shape, BF16),)
        + tuple(jax.ShapeDtypeStruct(item.shape, item.dtype) for item in kept),
        in_specs=[SMEM] * 3 + [HBM] * (5 + len(kept)),
        out_specs=(HBM,) * (1 + len(kept)),
        input_output_aliases={8 + i: 1 + i for i in range(len(kept))},
        scratch_shapes=[
            pltpu.VMEM(packed.shape, BF16),
            pltpu.VMEM((rows, width), BF16),
            pltpu.VMEM((rows, width), BF16),
            pltpu.VMEM((hidden, rows, TILE), F32),
            pltpu.VMEM((hidden, rows, TILE), BF16),
            pltpu.VMEM((hidden, rows, TILE), BF16),
            pltpu.VMEM((rows, width), BF16),
            pltpu.VMEM((rows, width), F32),
            pltpu.VMEM((2, rows, TILE), BF16),
            pltpu.SemaphoreType.DMA((1 + 2 * WEIGHT_CHUNKS,)),
            pltpu.SemaphoreType.DMA((3,)),
            pltpu.SemaphoreType.DMA((4,)),
        ],
        compiler_params=pltpu.CompilerParams(vmem_limit_bytes=VMEM_LIMIT),
        name="layer_backward",
    )(info, upq, dnq, cotangent, incoming, packed, xs, slope, *kept)


def grads_call(upq, dnq, xs, gs, act, gp, flat, blat, blocks):
    return pl.pallas_call(
        grads_kernel,
        out_shape=jax.ShapeDtypeStruct((blocks, PACKED, TILE), BF16),
        in_specs=[SMEM] * 2 + [VMEM] * 6,
        out_specs=VMEM,
        scratch_shapes=[pltpu.VMEM(xs.shape, BF16)],
        compiler_params=pltpu.CompilerParams(vmem_limit_bytes=VMEM_LIMIT),
        name="weight_grads",
    )(upq, dnq, xs, gs, act, gp, flat, blat)


def buffers(*shapes):
    return pl.pallas_call(
        lambda *refs: None,
        out_shape=tuple(jax.ShapeDtypeStruct(shape, BF16) for shape in shapes),
        out_specs=(HBM,) * len(shapes),
        name="buffers",
    )()


def rank_first(factor, groups):
    return factor.reshape(groups, TILE, RANK).swapaxes(1, 2).reshape(groups * RANK, TILE)


def rank_last(rows, groups):
    return rows.reshape(groups, RANK, TILE).swapaxes(1, 2).reshape(groups * TILE, RANK)


def gather(packed):
    return lax.all_gather(packed, "dp", axis=0)


def scatter_sum(terms):
    return lax.psum_scatter(terms, "dp", scatter_dimension=0)


def per_device(
    inputs, cotangent, up_blocks, up_index, up_left, up_right, down_blocks, down_index,
    down_left, down_right,
):
    sections = lax.axis_size("section")
    position = lax.axis_index("section")
    micro, rows, width = inputs.shape
    blocks = width // TILE
    hidden = blocks * PER_ROW
    upq, dnq = up_index[0, :, 1], down_index[0, :, 0]
    packed = gather(
        jnp.concatenate(
            [
                up_blocks[0].reshape(PER_ROW * TILE, TILE),
                down_blocks[0].reshape(PER_ROW * TILE, TILE),
                rank_first(up_left[0], 1),
                rank_first(up_right[0], PER_ROW),
                rank_first(down_left[0], PER_ROW),
                rank_first(down_right[0], 1),
            ]
        )
    )

    def info(number, first):
        live = (number >= 0) & (number < micro)
        slot = jnp.clip(number, 0, micro - 1)
        return jnp.stack([live, slot, first]).astype(jnp.int32)

    wide, tall, thin = (micro, rows, width), (micro, hidden, rows, TILE), (micro, 2, rows, TILE)
    xs, outs, act, slope, flat, gs, gp, blat = buffers(
        wide, wide, tall, tall, thin, wide, tall, thin
    )
    moments = micro + sections - 1
    incoming = inputs[0]
    for moment in range(moments):
        result, xs, outs, act, slope, flat = forward_call(
            info(moment - position, position == 0), upq, dnq, inputs, incoming, packed,
            (xs, outs, act, slope, flat),
        )
        route = [(s, s + 1) for s in range(sections - 1) if 0 <= moment - s < micro]
        if route:
            incoming = lax.ppermute(result, "section", route)

    incoming = cotangent[0]
    for moment in range(moments):
        result, gs, gp, blat = backward_call(
            info(moment - (sections - 1 - position), position == sections - 1),
            upq, dnq, cotangent, incoming, packed, xs, slope, (gs, gp, blat),
        )
        route = [
            (s, s - 1) for s in range(1, sections) if 0 <= moment - (sections - 1 - s) < micro
        ]
        if route:
            incoming = lax.ppermute(result, "section", route)

    terms = grads_call(upq, dnq, xs, gs, act, gp, flat, blat, blocks)
    total = scatter_sum(terms).astype(F32)
    return (
        outs[None],
        total[UP:DOWN].reshape(1, PER_ROW, TILE, TILE),
        rank_last(total[UP_LEFT:UP_RIGHT], 1)[None],
        rank_last(total[UP_RIGHT:DOWN_LEFT], PER_ROW)[None],
        total[DOWN:LOW].reshape(1, PER_ROW, TILE, TILE),
        rank_last(total[DOWN_LEFT:DOWN_RIGHT], PER_ROW)[None],
        rank_last(total[DOWN_RIGHT:PACKED], 1)[None],
    )


def solution(mesh):
    in_specs = (
        P(None, "dp", None),
        P(None, "dp", None),
        P("section", "dp", None, None),
        P("section", None, None),
        P("section", "dp", None),
        P("section", "dp", None),
        P("section", "dp", None, None),
        P("section", None, None),
        P("section", "dp", None),
        P("section", "dp", None),
    )
    out_specs = (
        P("section", None, "dp", None),
        P("section", "dp", None, None),
        P("section", "dp", None),
        P("section", "dp", None),
        P("section", "dp", None, None),
        P("section", "dp", None),
        P("section", "dp", None),
    )
    return jax.shard_map(
        per_device, mesh=mesh, in_specs=in_specs, out_specs=out_specs, check_vma=False
    )
```

```python
import math
from functools import partial

import jax
import jax.numpy as jnp
from jax import lax
from jax.experimental import pallas as pl
from jax.experimental.pallas import tpu as pltpu
from jax.sharding import Mesh
from jax.sharding import PartitionSpec as P

NORM_EPS = 1e-05
GELU_CUBIC = 0.044715
GELU_ROOT = math.sqrt(2.0 / math.pi)

TILE = 128
PER_ROW = 4
RANK = 16
MODEL = PER_ROW * TILE
HIDDEN = MODEL + RANK
SIDE = HIDDEN + PER_ROW * RANK
UP = 0
DOWN = 1
ALONG = 4
CORES = 2
SMALL_VMEM = 12 * 1024 * 1024
LAYER_VMEM = 12 * 1024 * 1024
F32 = jnp.float32
BF16 = jnp.bfloat16


def mm(left, right):
    return lax.dot_general(left, right, (((1,), (0,)), ((), ())), preferred_element_type=F32)


def mm_nt(left, right):
    return lax.dot_general(left, right, (((1,), (1,)), ((), ())), preferred_element_type=F32)


def mm_tn(left, right):
    return lax.dot_general(left, right, (((0,), (0,)), ((), ())), preferred_element_type=F32)


def lanes(pieces):
    return jnp.concatenate(pieces, axis=1)


def low_rows(side, index):
    return lanes(
        [side[index, HIDDEN + RANK * i : HIDDEN + RANK * (i + 1), :] for i in range(PER_ROW)]
    )


def normalised(x_ref):
    xf = x_ref[...].astype(F32)
    scaling = lax.rsqrt(jnp.mean(xf * xf, axis=-1, keepdims=True) + NORM_EPS)
    return xf, scaling


def slot_at(number, micro):
    live = (number >= 0) & (number < micro)
    return live, jnp.clip(number, 0, micro - 1)


def forward_kernel(
    moment, place, upq, dnq, inputs, incoming, wu, wd, xs_in, outs_in, act_in, slope_in, lat_in,
    y, xs, outs, act, slope, lat,
    pre,
):
    position = place[3]
    live, slot = slot_at(moment - 2 * position, inputs.shape[0])
    blocks = wu.shape[0]
    hidden = pre.shape[0]
    rows = y.shape[0]

    @pl.when(live)
    def _():
        @pl.when(position == 0)
        def _():
            xs[slot] = inputs[slot]

        @pl.when(position != 0)
        def _():
            xs[slot] = incoming[...]

        x = xs[slot]
        xf, scaling = normalised(x)
        normed = (xf * scaling).astype(BF16)
        up_latent = jnp.zeros((rows, RANK), F32)
        for j in range(0, blocks, 2):
            up_latent += mm_nt(
                normed[:, j * TILE : (j + 2) * TILE],
                lanes([wu[j + i, MODEL:HIDDEN, :] for i in range(2)]),
            )
        up_latent = up_latent.astype(BF16)
        lat[slot, 0, :, 0:RANK] = up_latent
        for p in range(blocks):
            low = mm(up_latent, low_rows(wu, p))
            for i in range(PER_ROW):
                pre[PER_ROW * p + i] = low[:, i * TILE : (i + 1) * TILE]
        for p in range(blocks):
            piece = lanes([wu[p, i * TILE : (i + 1) * TILE, :] for i in range(PER_ROW)])
            product = mm(normed[:, p * TILE : (p + 1) * TILE], piece)
            where = [upq[PER_ROW * p + i] for i in range(PER_ROW)]
            sums = [pre[q] + product[:, i * TILE : (i + 1) * TILE] for i, q in enumerate(where)]
            for q, value in zip(where, sums):
                pre[q] = value

        def gelu(q, carry):
            u = pre[q]
            square = u * u
            bend = jnp.tanh(u * (GELU_ROOT + GELU_ROOT * GELU_CUBIC * square))
            half = 0.5 + 0.5 * bend
            act[slot, q] = (u * half).astype(BF16)
            inner = 0.5 * GELU_ROOT + 1.5 * GELU_ROOT * GELU_CUBIC * square
            slopes = half + (u * inner) * (1.0 - bend * bend)
            slope[slot, q] = slopes.astype(BF16)
            return carry

        lax.fori_loop(0, hidden, gelu, 0, unroll=8)
        down_latent = jnp.zeros((rows, RANK), F32)
        for p in range(blocks):
            down_latent += mm_nt(
                lanes([act[slot, PER_ROW * p + i] for i in range(PER_ROW)]),
                low_rows(wd, p),
            )
        down_latent = down_latent.astype(BF16)
        lat[slot, 1, :, 0:RANK] = down_latent
        for p in range(blocks):
            left = lanes([act[slot, dnq[PER_ROW * p + i]] for i in range(PER_ROW)])
            product = mm(left, wd[p, 0:MODEL, :])
            product += mm(down_latent, wd[p, MODEL:HIDDEN, :])
            cols = slice(p * TILE, (p + 1) * TILE)
            result = (x[:, cols].astype(F32) + product).astype(BF16)
            y[:, cols] = result
            outs[slot, :, cols] = result


def backward_kernel(
    moment, sections, place, upq, dnq, cotangent, incoming, wu, wd, xs, gs_in, slope, lat_in,
    y, gs, gp, lat,
    ga, norm,
):
    position = place[3]
    live, slot = slot_at(moment - 2 * (sections - 1 - position), cotangent.shape[0])
    blocks = wu.shape[0]
    hidden = ga.shape[0]
    rows = y.shape[0]

    @pl.when(live)
    def _():
        @pl.when(position == sections - 1)
        def _():
            gs[slot] = cotangent[slot]

        @pl.when(position != sections - 1)
        def _():
            gs[slot] = incoming[...]

        g = gs[slot]
        down = jnp.zeros((rows, RANK), F32)
        for j in range(0, blocks, 2):
            down += mm_nt(
                g[:, j * TILE : (j + 2) * TILE],
                lanes([wd[j + i, MODEL:HIDDEN, :] for i in range(2)]),
            )
        down = down.astype(BF16)
        lat[slot, 1, :, 0:RANK] = down
        for p in range(blocks):
            low = mm(down, low_rows(wd, p))
            for i in range(PER_ROW):
                ga[PER_ROW * p + i] = low[:, i * TILE : (i + 1) * TILE]
        for p in range(blocks):
            product = mm_nt(g[:, p * TILE : (p + 1) * TILE], wd[p, 0:MODEL, :])
            where = [dnq[PER_ROW * p + i] for i in range(PER_ROW)]
            sums = [ga[q] + product[:, i * TILE : (i + 1) * TILE] for i, q in enumerate(where)]
            for q, value in zip(where, sums):
                ga[q] = value

        def slopes(q, carry):
            gp[slot, q] = (ga[q] * slope[slot, q].astype(F32)).astype(BF16)
            return carry

        lax.fori_loop(0, hidden, slopes, 0, unroll=8)
        up = jnp.zeros((rows, RANK), F32)
        for p in range(blocks):
            up += mm_nt(
                lanes([gp[slot, PER_ROW * p + i] for i in range(PER_ROW)]),
                low_rows(wu, p),
            )
        up = up.astype(BF16)
        lat[slot, 0, :, 0:RANK] = up
        xf, scaling = normalised(xs[slot])
        along = jnp.zeros((rows, TILE), F32)
        for p in range(blocks):
            left = lanes([gp[slot, upq[PER_ROW * p + i]] for i in range(PER_ROW)])
            piece = lanes([wu[p, i * TILE : (i + 1) * TILE, :] for i in range(PER_ROW)])
            product = mm_nt(left, piece)
            product += mm(up, wu[p, MODEL:HIDDEN, :])
            cols = slice(p * TILE, (p + 1) * TILE)
            norm[:, cols] = product
            along += product * (xf[:, cols] * scaling)
        mean = jnp.sum(along, axis=-1, keepdims=True) * (1.0 / (blocks * TILE))
        y[...] = (
            g.astype(F32) + scaling * (norm[...] - (xf * scaling) * mean)
        ).astype(BF16)


def place_of(place, p, side):
    dz = lax.rem(p // (ALONG * CORES) - place[0] + ALONG, ALONG)
    dy = lax.rem(lax.rem(p // CORES, ALONG) - place[1] + ALONG, ALONG)
    other = lax.rem(lax.rem(p, CORES) + side, CORES)
    return (dz, dy, other) if side == UP else (dy, dz, other)


def column(ref, p):
    tokens = ref.shape[0] * ref.shape[1]
    return ref[:, :, pl.ds(pl.multiple_of(p * TILE, TILE), TILE)].reshape(tokens, TILE)


def of_hidden(ref, q):
    return ref[:, pl.ds(q, 1)].reshape(ref.shape[0] * ref.shape[2], TILE)


def latent(ref, kind):
    return ref[:, kind, :, 0:RANK].reshape(ref.shape[0] * ref.shape[2], RANK)


def put_low(out, where, low):
    for i in range(PER_ROW):
        rows = slice(HIDDEN + RANK * i, HIDDEN + RANK * (i + 1))
        out[(*where, rows, slice(None))] = low[:, i * TILE : (i + 1) * TILE].astype(BF16)


def down_grads(place, dnq, gs, act, flat, blat, out):
    blocks = gs.shape[2] // TILE
    down_latent, grad_down_latent = latent(flat, 1), latent(blat, 1)

    def one(p, carry):
        where = place_of(place, p, DOWN)
        g = column(gs, p)
        for i in range(PER_ROW):
            product = mm_tn(of_hidden(act, dnq[PER_ROW * p + i]), g)
            out[(*where, slice(i * TILE, (i + 1) * TILE), slice(None))] = product.astype(BF16)
        out[(*where, slice(MODEL, HIDDEN), slice(None))] = mm_tn(down_latent, g).astype(BF16)
        here = lanes([of_hidden(act, PER_ROW * p + i) for i in range(PER_ROW)])
        put_low(out, where, mm_tn(grad_down_latent, here))
        return carry

    lax.fori_loop(0, blocks, one, 0, unroll=2)


def up_grads(place, upq, xs, gp, flat, blat, out, normed):
    blocks = xs.shape[2] // TILE
    xf, scaling = normalised(xs)
    normed[...] = (xf * scaling).astype(BF16)
    up_latent, grad_up_latent = latent(flat, 0), latent(blat, 0)

    def one(p, carry):
        where = place_of(place, p, UP)
        n = column(normed, p)
        there = lanes([of_hidden(gp, upq[PER_ROW * p + i]) for i in range(PER_ROW)])
        product = mm_tn(n, there)
        for i in range(PER_ROW):
            out[(*where, slice(i * TILE, (i + 1) * TILE), slice(None))] = product[
                :, i * TILE : (i + 1) * TILE
            ].astype(BF16)
        out[(*where, slice(MODEL, HIDDEN), slice(None))] = mm_tn(grad_up_latent, n).astype(BF16)
        here = lanes([of_hidden(gp, PER_ROW * p + i) for i in range(PER_ROW)])
        put_low(out, where, mm_tn(up_latent, here))
        return carry

    lax.fori_loop(0, blocks, one, 0, unroll=2)


def grads_kernel(keep, place, upq, dnq, xs, gs, act, gp, flat, blat, out, normed):
    core = place[2]

    @pl.when(core == (UP if keep else DOWN))
    def _():
        up_grads(place, upq, xs, gp, flat, blat, out, normed)

    @pl.when(core == (DOWN if keep else UP))
    def _():
        down_grads(place, dnq, gs, act, flat, blat, out)


def pack_kernel(
    place, up_blocks, up_left, up_right, down_blocks, down_left, down_right, mine, other
):
    for side, tiles, model, hidden in (
        (UP, up_blocks, up_left, up_right),
        (DOWN, down_blocks, down_right, down_left),
    ):
        for out, core in ((mine, side), (other, 1 - side)):

            @pl.when(place[2] == core)
            def _():
                for i in range(PER_ROW):
                    out[i * TILE : (i + 1) * TILE, :] = tiles[i]
                out[MODEL:HIDDEN, :] = model[...]
                for i in range(PER_ROW):
                    rows = slice(HIDDEN + RANK * i, HIDDEN + RANK * (i + 1))
                    out[rows, :] = hidden[:, i * TILE : (i + 1) * TILE]


def stack_kernel(*refs):
    for d, piece in enumerate(refs[:-1]):
        refs[-1][d] = piece[...]


def spread_kernel(place, *refs):
    mine, other, sides = refs[:ALONG], refs[ALONG : 2 * ALONG], refs[2 * ALONG :]
    z, y, core = place[0], place[1], place[2]
    for side, out in zip((UP, DOWN), sides):
        for pieces, holder in ((mine, side), (other, 1 - side)):

            @pl.when(core == holder)
            def _():
                for outer in range(ALONG):
                    for inner in range(ALONG):
                        dz, dy = (outer, inner) if side == UP else (inner, outer)
                        back_z = lax.rem(z - dz + ALONG, ALONG)
                        back_y = lax.rem(y - dy + ALONG, ALONG)
                        chip = back_z * ALONG + back_y
                        for far in range(CORES):
                            out[chip * CORES + (side + far) % CORES] = pieces[outer][inner, far]


def add_cores_kernel(mine, came, *outs):
    for outer, out in enumerate(outs):
        for inner in range(ALONG):
            total = mine[outer, inner].astype(F32) + came[outer, inner].astype(F32)
            out[inner] = total.astype(BF16)


def add_far_kernel(*refs):
    terms, outs = refs[:ALONG], refs[ALONG:]
    for inner, out in enumerate(outs):
        total = terms[0][inner].astype(F32)
        for came in terms[1:]:
            total += came[inner].astype(F32)
        out[...] = total.astype(BF16)


def add_last_kernel(*refs):
    terms, outs = refs[:ALONG], refs[ALONG:]
    for far, out in enumerate(outs):
        total = terms[0][far].astype(F32)
        for came in terms[1:]:
            total += came[far].astype(F32)
        out[...] = total


def finish_kernel(place, mine, other, *outs):
    for side, (tiles, model, hidden) in ((UP, outs[:3]), (DOWN, outs[3:])):
        for total, core in ((mine, side), (other, 1 - side)):

            @pl.when(place[2] == core)
            def _():
                for i in range(PER_ROW):
                    tiles[i] = total[i * TILE : (i + 1) * TILE, :]
                model[...] = total[MODEL:HIDDEN, :]
                for i in range(PER_ROW):
                    rows = slice(HIDDEN + RANK * i, HIDDEN + RANK * (i + 1))
                    hidden[:, i * TILE : (i + 1) * TILE] = total[rows, :]


SMEM = pl.BlockSpec(memory_space=pltpu.SMEM)
VMEM = pl.BlockSpec(memory_space=pltpu.VMEM)
HBM = pl.BlockSpec(memory_space=pl.ANY)


def near(array):
    return pltpu.with_memory_space_constraint(array, pltpu.VMEM)


def forward_call(moment, place, upq, dnq, inputs, incoming, packed, kept):
    rows, width = incoming.shape
    hidden = packed[0].shape[0] * PER_ROW
    return pl.pallas_call(
        partial(forward_kernel, moment),
        out_shape=(pltpu.VMEM(incoming.shape, BF16),)
        + tuple(pltpu.VMEM(item.shape, item.dtype) for item in kept),
        in_specs=[SMEM] * 3 + [VMEM] * (4 + len(kept)),
        out_specs=(VMEM,) * (1 + len(kept)),
        input_output_aliases={7 + i: 1 + i for i in range(len(kept))},
        scratch_shapes=[pltpu.VMEM((hidden, rows, TILE), F32)],
        compiler_params=pltpu.CompilerParams(vmem_limit_bytes=LAYER_VMEM),
        cost_estimate=pl.CostEstimate(flops=10**9, bytes_accessed=10**7, transcendentals=0),
        name="layer_forward",
    )(place, upq, dnq, *map(near, (inputs, incoming, *packed, *kept)))


def backward_call(moment, sections, place, upq, dnq, cotangent, incoming, packed, xs, kept):
    rows, width = incoming.shape
    hidden = packed[0].shape[0] * PER_ROW
    return pl.pallas_call(
        partial(backward_kernel, moment, sections),
        out_shape=(pltpu.VMEM(incoming.shape, BF16),)
        + tuple(pltpu.VMEM(item.shape, item.dtype) for item in kept),
        in_specs=[SMEM] * 3 + [VMEM] * (5 + len(kept)),
        out_specs=(VMEM,) * (1 + len(kept)),
        input_output_aliases={8 + i: 1 + i for i in range(len(kept))},
        scratch_shapes=[pltpu.VMEM((hidden, rows, TILE), F32), pltpu.VMEM((rows, width), F32)],
        compiler_params=pltpu.CompilerParams(vmem_limit_bytes=LAYER_VMEM),
        cost_estimate=pl.CostEstimate(flops=10**9, bytes_accessed=10**7, transcendentals=0),
        name="layer_backward",
    )(place, upq, dnq, *map(near, (cotangent, incoming, *packed, xs, *kept)))


def near_call(kernel, name, shapes, scalars, arrays, scratch=(), far=False):
    specs = [SMEM] * len(scalars) + [VMEM] * len(arrays)
    made = jax.ShapeDtypeStruct if far else pltpu.VMEM
    return pl.pallas_call(
        kernel,
        out_shape=tuple(made(*shape) for shape in shapes),
        in_specs=specs,
        out_specs=(VMEM,) * len(shapes),
        scratch_shapes=list(scratch),
        compiler_params=pltpu.CompilerParams(vmem_limit_bytes=SMALL_VMEM),
        name=name,
    )(*scalars, *map(near, arrays))


def dp_send(value, *steps):
    def index(z, y, c):
        return ((z % ALONG) * ALONG + y % ALONG) * CORES + c % CORES

    route = []
    for z in range(ALONG):
        for y in range(ALONG):
            for c in range(CORES):
                dz, dy, dc = steps[c % len(steps)]
                route.append((index(z, y, c), index(z + dz, y + dy, c + dc)))
    return lax.ppermute(value, "dp", route)


def swap_cores(value):
    return dp_send(value, (0, 0, 1))


def along_first(value, d):
    return dp_send(value, (0, d, 0), (d, 0, 0))


def along_second(value, d):
    return dp_send(value, (d, 0, 0), (0, d, 0))


FAR = range(1, ALONG)


def gather(place, mine, other):
    side = mine.shape
    pair = near_call(
        stack_kernel, "pair", [((CORES, *side), BF16)], (), (mine, swap_cores(other))
    )[0]
    pairs = [pair] + [along_first(pair, d) for d in FAR]
    line = near_call(stack_kernel, "line", [((ALONG, CORES, *side), BF16)], (), pairs)[0]
    lines = [line] + [along_second(line, d) for d in FAR]
    others = [swap_cores(piece) for piece in lines]
    full = ((CORES * ALONG * ALONG, *side), BF16)
    return near_call(spread_kernel, "spread", (full, full), (place,), lines + others)


def scatter_sum(place, keep, give):
    side = keep.shape[3:]
    line, pair = ((ALONG, CORES, *side), BF16), ((CORES, *side), BF16)
    came = swap_cores(give)
    lines = near_call(add_cores_kernel, "add_cores", [line] * ALONG, (), (keep, came))
    terms = [lines[0]] + [along_second(lines[d], d) for d in FAR]
    pairs = near_call(add_far_kernel, "add_far", [pair] * ALONG, (), terms)
    terms = [pairs[0]] + [along_first(pairs[d], d) for d in FAR]
    mine, other = near_call(add_last_kernel, "add_last", [(side, F32)] * CORES, (), terms)
    three = (((PER_ROW, TILE, TILE), F32), ((RANK, TILE), F32), ((RANK, MODEL), F32))
    return near_call(
        finish_kernel, "finish", three + three, (place,), (mine, swap_cores(other)), far=True
    )


def buffers(after, *shapes):
    shapes = [(shape, BF16) for shape in shapes]
    return near_call(lambda *refs: None, "buffers", shapes, (), (after,))


def per_device(
    inputs, cotangent, up_blocks, up_index, up_left, up_right, down_blocks, down_index,
    down_left, down_right,
):
    sections = lax.axis_size("section")
    micro, rows, width = inputs.shape
    hidden = width // TILE * PER_ROW
    rank = lax.axis_index("dp")
    place = jnp.stack(
        [
            rank // (ALONG * CORES),
            rank // CORES % ALONG,
            rank % CORES,
            lax.axis_index("section"),
        ]
    ).astype(jnp.int32)
    place, upq, dnq = lax.optimization_barrier((place, up_index[0, :, 1], down_index[0, :, 0]))
    side = ((SIDE, TILE), BF16)
    factors = [item[0].T for item in (up_left, up_right, down_left, down_right)]
    packed = gather(
        place,
        *near_call(
            pack_kernel,
            "pack",
            (side, side),
            (place,),
            (up_blocks[0], *factors[:2], down_blocks[0], *factors[2:]),
        ),
    )

    wide, tall, thin = (micro, rows, width), (micro, hidden, rows, TILE), (micro, 2, rows, TILE)
    xs, outs, act, slope, flat, arrived, travelling = buffers(
        packed[0], wide, wide, tall, tall, thin, (rows, width), (rows, width)
    )
    moments = micro + 2 * (sections - 1)
    for moment in range(moments):
        result, xs, outs, act, slope, flat = forward_call(
            moment, place, upq, dnq, inputs, arrived, packed, (xs, outs, act, slope, flat)
        )
        route = [(s, s + 1) for s in range(sections - 1) if 0 <= moment - 2 * s < micro]
        arrived = travelling
        if route:
            travelling = lax.ppermute(result, "section", route)

    gs, blat, arrived, travelling = buffers(act, wide, thin, (rows, width), (rows, width))
    gp = slope
    for moment in range(moments):
        result, gs, gp, blat = backward_call(
            moment, sections, place, upq, dnq, cotangent, arrived, packed, xs, (gs, gp, blat)
        )
        route = [
            (s, s - 1) for s in range(1, sections) if 0 <= moment - 2 * (sections - 1 - s) < micro
        ]
        arrived = travelling
        if route:
            travelling = lax.ppermute(result, "section", route)

    terms = [
        near_call(
            partial(grads_kernel, keep),
            "grads",
            [((ALONG, ALONG, CORES, SIDE, TILE), BF16)],
            (place, upq, dnq),
            (xs, gs, act, gp, flat, blat),
            (pltpu.VMEM(wide, BF16),),
        )[0]
        for keep in (False, True)
    ]
    up_grad, up_left_grad, up_right_grad, down_grad, down_right_grad, down_left_grad = scatter_sum(
        place, terms[1], terms[0]
    )
    return (
        outs[None],
        up_grad[None],
        up_left_grad.T[None],
        up_right_grad.T[None],
        down_grad[None],
        down_left_grad.T[None],
        down_right_grad.T[None],
    )


def solution(mesh):
    in_specs = (
        P(None, "dp", None),
        P(None, "dp", None),
        P("section", "dp", None, None),
        P("section", None, None),
        P("section", "dp", None),
        P("section", "dp", None),
        P("section", "dp", None, None),
        P("section", None, None),
        P("section", "dp", None),
        P("section", "dp", None),
    )
    out_specs = (
        P("section", None, "dp", None),
        P("section", "dp", None, None),
        P("section", "dp", None),
        P("section", "dp", None),
        P("section", "dp", None, None),
        P("section", "dp", None),
        P("section", "dp", None),
    )
    return jax.shard_map(
        per_device, mesh=mesh, in_specs=in_specs, out_specs=out_specs, check_vma=False
    )
```

```python
import math
from functools import partial

import jax
import jax.numpy as jnp
from jax import lax
from jax.experimental import pallas as pl
from jax.experimental.pallas import tpu as pltpu
from jax.sharding import Mesh
from jax.sharding import PartitionSpec as P

NORM_EPS = 1e-05
GELU_CUBIC = 0.044715
GELU_ROOT = math.sqrt(2.0 / math.pi)

TILE = 128
PER_ROW = 4
RANK = 16
MODEL = PER_ROW * TILE
HIDDEN = MODEL + RANK
SIDE = HIDDEN + PER_ROW * RANK
UP = 0
DOWN = 1
ALONG = 4
CORES = 2
SMALL_VMEM = 12 * 1024 * 1024
UNROLL = 16
MOMENT_GROUP = 4
LAYER_VMEM = 12 * 1024 * 1024
F32 = jnp.float32
BF16 = jnp.bfloat16


def mm(left, right):
    return lax.dot_general(left, right, (((1,), (0,)), ((), ())), preferred_element_type=F32)


def mm_nt(left, right):
    return lax.dot_general(left, right, (((1,), (1,)), ((), ())), preferred_element_type=F32)


def mm_tn(left, right):
    return lax.dot_general(left, right, (((0,), (0,)), ((), ())), preferred_element_type=F32)


def lanes(pieces):
    return jnp.concatenate(pieces, axis=1)


def low_rows(side, index):
    return lanes(
        [side[index, HIDDEN + RANK * i : HIDDEN + RANK * (i + 1), :] for i in range(PER_ROW)]
    )


def normalised(x_ref):
    xf = x_ref[...].astype(F32)
    scaling = lax.rsqrt(jnp.mean(xf * xf, axis=-1, keepdims=True) + NORM_EPS)
    return xf, scaling


def slot_at(number, micro):
    live = (number >= 0) & (number < micro)
    return live, jnp.clip(number, 0, micro - 1)


def forward_kernel(
    moment, place, upq, dnq, inputs, incoming, wu, wd, xs_in, outs_in, act_in, slope_in, lat_in,
    y, xs, outs, act, slope, lat,
    pre, nv,
):
    position = place[3]
    live, slot = slot_at(moment - 2 * position, inputs.shape[0])
    blocks = wu.shape[0]
    hidden = pre.shape[0]
    rows = y.shape[0]

    @pl.when(live)
    def _():
        @pl.when(position == 0)
        def _():
            xs[slot] = inputs[slot]

        @pl.when(position != 0)
        def _():
            xs[slot] = incoming[...]

        xf, scaling = normalised(xs.at[slot])
        normed = (xf * scaling).astype(BF16)
        for p in range(blocks):
            nv[p] = normed[:, p * TILE : (p + 1) * TILE]

        def to_latent(j, total):
            pair = lanes([nv[2 * j], nv[2 * j + 1]])
            factor = lanes([wu[2 * j + i, MODEL:HIDDEN, :] for i in range(2)])
            return total + mm_nt(pair, factor)

        none = jnp.zeros((rows, RANK), F32)
        up_latent = lax.fori_loop(0, blocks // 2, to_latent, none, unroll=UNROLL // 2).astype(BF16)
        lat[slot, 0, :, 0:RANK] = up_latent

        def low_rank(p, carry):
            low = mm(up_latent, low_rows(wu, p))
            for i in range(PER_ROW):
                pre[PER_ROW * p + i] = low[:, i * TILE : (i + 1) * TILE]
            return carry

        lax.fori_loop(0, blocks, low_rank, 0, unroll=UNROLL)

        def up_blocks(p, carry):
            product = mm(nv[p], lanes([wu[p, i * TILE : (i + 1) * TILE, :] for i in range(PER_ROW)]))
            where = [upq[PER_ROW * p + i] for i in range(PER_ROW)]
            sums = [pre[q] + product[:, i * TILE : (i + 1) * TILE] for i, q in enumerate(where)]
            for q, value in zip(where, sums):
                pre[q] = value
            return carry

        lax.fori_loop(0, blocks, up_blocks, 0, unroll=UNROLL)

        def gelu(q, carry):
            u = pre[q]
            square = u * u
            bend = jnp.tanh(u * (GELU_ROOT + GELU_ROOT * GELU_CUBIC * square))
            half = 0.5 + 0.5 * bend
            act[slot, q] = (u * half).astype(BF16)
            inner = 0.5 * GELU_ROOT + 1.5 * GELU_ROOT * GELU_CUBIC * square
            slopes = half + (u * inner) * (1.0 - bend * bend)
            slope[slot, q] = slopes.astype(BF16)
            return carry

        lax.fori_loop(0, hidden, gelu, 0, unroll=8)

        def from_hidden(p, total):
            return total + mm_nt(
                lanes([act[slot, PER_ROW * p + i] for i in range(PER_ROW)]), low_rows(wd, p)
            )

        down_latent = lax.fori_loop(0, blocks, from_hidden, none, unroll=UNROLL).astype(BF16)
        lat[slot, 1, :, 0:RANK] = down_latent

        def down_blocks(p, carry):
            left = lanes([act[slot, dnq[PER_ROW * p + i]] for i in range(PER_ROW)])
            product = mm(left, wd[p, 0:MODEL, :])
            product += mm(down_latent, wd[p, MODEL:HIDDEN, :])
            cols = pl.ds(pl.multiple_of(p * TILE, TILE), TILE)
            result = (xs[slot, :, cols].astype(F32) + product).astype(BF16)
            y[:, cols] = result
            outs[slot, :, cols] = result
            return carry

        lax.fori_loop(0, blocks, down_blocks, 0, unroll=UNROLL)


def backward_kernel(
    moment, sections, place, upq, dnq, cotangent, incoming, wu, wd, xs, gs_in, slope, lat_in,
    y, gs, gp, lat,
    ga, norm, unit,
):
    position = place[3]
    live, slot = slot_at(moment - 2 * (sections - 1 - position), cotangent.shape[0])
    blocks = wu.shape[0]
    hidden = ga.shape[0]
    rows = y.shape[0]

    @pl.when(live)
    def _():
        @pl.when(position == sections - 1)
        def _():
            gs[slot] = cotangent[slot]

        @pl.when(position != sections - 1)
        def _():
            gs[slot] = incoming[...]

        def columns(p, count=1):
            return pl.ds(pl.multiple_of(p * TILE, TILE), count * TILE)

        def to_latent(j, total):
            factor = lanes([wd[2 * j + i, MODEL:HIDDEN, :] for i in range(2)])
            return total + mm_nt(gs[slot, :, columns(2 * j, 2)], factor)

        none = jnp.zeros((rows, RANK), F32)
        down = lax.fori_loop(0, blocks // 2, to_latent, none, unroll=UNROLL // 2).astype(BF16)
        lat[slot, 1, :, 0:RANK] = down

        def low_rank(p, carry):
            low = mm(down, low_rows(wd, p))
            for i in range(PER_ROW):
                ga[PER_ROW * p + i] = low[:, i * TILE : (i + 1) * TILE]
            return carry

        lax.fori_loop(0, blocks, low_rank, 0, unroll=UNROLL)

        def down_blocks(p, carry):
            product = mm_nt(gs[slot, :, columns(p)], wd[p, 0:MODEL, :])
            where = [dnq[PER_ROW * p + i] for i in range(PER_ROW)]
            sums = [ga[q] + product[:, i * TILE : (i + 1) * TILE] for i, q in enumerate(where)]
            for q, value in zip(where, sums):
                ga[q] = value
            return carry

        lax.fori_loop(0, blocks, down_blocks, 0, unroll=UNROLL)

        def slopes(q, carry):
            gp[slot, q] = (ga[q] * slope[slot, q].astype(F32)).astype(BF16)
            return carry

        lax.fori_loop(0, hidden, slopes, 0, unroll=8)

        def from_hidden(p, total):
            return total + mm_nt(
                lanes([gp[slot, PER_ROW * p + i] for i in range(PER_ROW)]), low_rows(wu, p)
            )

        up = lax.fori_loop(0, blocks, from_hidden, none, unroll=UNROLL).astype(BF16)
        lat[slot, 0, :, 0:RANK] = up
        xf, scaling = normalised(xs.at[slot])
        unit[...] = xf * scaling

        def up_blocks(p, along):
            left = lanes([gp[slot, upq[PER_ROW * p + i]] for i in range(PER_ROW)])
            piece = lanes([wu[p, i * TILE : (i + 1) * TILE, :] for i in range(PER_ROW)])
            product = mm_nt(left, piece)
            product += mm(up, wu[p, MODEL:HIDDEN, :])
            norm[:, columns(p)] = product
            return along + product * unit[:, columns(p)]

        along = jnp.zeros((rows, TILE), F32)
        along = lax.fori_loop(0, blocks, up_blocks, along, unroll=UNROLL)
        mean = jnp.sum(along, axis=-1, keepdims=True) * (1.0 / (blocks * TILE))
        y[...] = (
            gs[slot].astype(F32) + scaling * (norm[...] - unit[...] * mean)
        ).astype(BF16)


def place_of(place, p, side):
    dz = lax.rem(p // (ALONG * CORES) - place[0] + ALONG, ALONG)
    dy = lax.rem(lax.rem(p // CORES, ALONG) - place[1] + ALONG, ALONG)
    other = lax.rem(lax.rem(p, CORES) + side, CORES)
    return (dz, dy, other) if side == UP else (dy, dz, other)


def column(ref, p):
    tokens = ref.shape[0] * ref.shape[1]
    return ref[:, :, pl.ds(pl.multiple_of(p * TILE, TILE), TILE)].reshape(tokens, TILE)


def of_hidden(ref, q):
    return ref[:, pl.ds(q, 1)].reshape(ref.shape[0] * ref.shape[2], TILE)


def latent(ref, kind):
    return ref[:, kind, :, 0:RANK].reshape(ref.shape[0] * ref.shape[2], RANK)


def put_low(out, where, low):
    for i in range(PER_ROW):
        rows = slice(HIDDEN + RANK * i, HIDDEN + RANK * (i + 1))
        out[(*where, rows, slice(None))] = low[:, i * TILE : (i + 1) * TILE].astype(BF16)


def down_grads(place, dnq, gs, act, flat, blat, out):
    blocks = gs.shape[2] // TILE
    down_latent, grad_down_latent = latent(flat, 1), latent(blat, 1)

    def one(p, carry):
        where = place_of(place, p, DOWN)
        g = column(gs, p)
        for i in range(PER_ROW):
            product = mm_tn(of_hidden(act, dnq[PER_ROW * p + i]), g)
            out[(*where, slice(i * TILE, (i + 1) * TILE), slice(None))] = product.astype(BF16)
        out[(*where, slice(MODEL, HIDDEN), slice(None))] = mm_tn(down_latent, g).astype(BF16)
        here = lanes([of_hidden(act, PER_ROW * p + i) for i in range(PER_ROW)])
        put_low(out, where, mm_tn(grad_down_latent, here))
        return carry

    lax.fori_loop(0, blocks, one, 0, unroll=2)


def up_grads(place, upq, xs, gp, flat, blat, out, normed):
    blocks = xs.shape[2] // TILE
    xf, scaling = normalised(xs)
    normed[...] = (xf * scaling).astype(BF16)
    up_latent, grad_up_latent = latent(flat, 0), latent(blat, 0)

    def one(p, carry):
        where = place_of(place, p, UP)
        n = column(normed, p)
        there = lanes([of_hidden(gp, upq[PER_ROW * p + i]) for i in range(PER_ROW)])
        product = mm_tn(n, there)
        for i in range(PER_ROW):
            out[(*where, slice(i * TILE, (i + 1) * TILE), slice(None))] = product[
                :, i * TILE : (i + 1) * TILE
            ].astype(BF16)
        out[(*where, slice(MODEL, HIDDEN), slice(None))] = mm_tn(grad_up_latent, n).astype(BF16)
        here = lanes([of_hidden(gp, PER_ROW * p + i) for i in range(PER_ROW)])
        put_low(out, where, mm_tn(up_latent, here))
        return carry

    lax.fori_loop(0, blocks, one, 0, unroll=2)


def grads_kernel(keep, place, upq, dnq, xs, gs, act, gp, flat, blat, out, normed):
    core = place[2]

    @pl.when(core == (UP if keep else DOWN))
    def _():
        up_grads(place, upq, xs, gp, flat, blat, out, normed)

    @pl.when(core == (DOWN if keep else UP))
    def _():
        down_grads(place, dnq, gs, act, flat, blat, out)


def pack_kernel(
    place, up_blocks, up_left, up_right, down_blocks, down_left, down_right, mine, other
):
    for side, tiles, model, hidden in (
        (UP, up_blocks, up_left, up_right),
        (DOWN, down_blocks, down_right, down_left),
    ):
        for out, core in ((mine, side), (other, 1 - side)):

            @pl.when(place[2] == core)
            def _():
                for i in range(PER_ROW):
                    out[i * TILE : (i + 1) * TILE, :] = tiles[i]
                out[MODEL:HIDDEN, :] = model[...]
                for i in range(PER_ROW):
                    rows = slice(HIDDEN + RANK * i, HIDDEN + RANK * (i + 1))
                    out[rows, :] = hidden[:, i * TILE : (i + 1) * TILE]


def stack_kernel(*refs):
    for d, piece in enumerate(refs[:-1]):
        refs[-1][d] = piece[...]


def spread_kernel(place, *refs):
    mine, other, sides = refs[:ALONG], refs[ALONG : 2 * ALONG], refs[2 * ALONG :]
    z, y, core = place[0], place[1], place[2]
    for side, out in zip((UP, DOWN), sides):
        for pieces, holder in ((mine, side), (other, 1 - side)):

            @pl.when(core == holder)
            def _():
                for outer in range(ALONG):
                    for inner in range(ALONG):
                        dz, dy = (outer, inner) if side == UP else (inner, outer)
                        back_z = lax.rem(z - dz + ALONG, ALONG)
                        back_y = lax.rem(y - dy + ALONG, ALONG)
                        chip = back_z * ALONG + back_y
                        for far in range(CORES):
                            out[chip * CORES + (side + far) % CORES] = pieces[outer][inner, far]


def add_cores_kernel(mine, came, *outs):
    for outer, out in enumerate(outs):
        for inner in range(ALONG):
            total = mine[outer, inner].astype(F32) + came[outer, inner].astype(F32)
            out[inner] = total.astype(BF16)


def add_far_kernel(*refs):
    terms, outs = refs[:ALONG], refs[ALONG:]
    for inner, out in enumerate(outs):
        total = terms[0][inner].astype(F32)
        for came in terms[1:]:
            total += came[inner].astype(F32)
        out[...] = total.astype(BF16)


def add_last_kernel(*refs):
    terms, outs = refs[:ALONG], refs[ALONG:]
    for far, out in enumerate(outs):
        total = terms[0][far].astype(F32)
        for came in terms[1:]:
            total += came[far].astype(F32)
        out[...] = total


def finish_kernel(place, mine, other, *outs):
    for side, (tiles, model, hidden) in ((UP, outs[:3]), (DOWN, outs[3:])):
        for total, core in ((mine, side), (other, 1 - side)):

            @pl.when(place[2] == core)
            def _():
                for i in range(PER_ROW):
                    tiles[i] = total[i * TILE : (i + 1) * TILE, :]
                model[...] = total[MODEL:HIDDEN, :]
                for i in range(PER_ROW):
                    rows = slice(HIDDEN + RANK * i, HIDDEN + RANK * (i + 1))
                    hidden[:, i * TILE : (i + 1) * TILE] = total[rows, :]


SMEM = pl.BlockSpec(memory_space=pltpu.SMEM)
VMEM = pl.BlockSpec(memory_space=pltpu.VMEM)
HBM = pl.BlockSpec(memory_space=pl.ANY)


def near(array):
    return pltpu.with_memory_space_constraint(array, pltpu.VMEM)


def forward_call(moment, place, upq, dnq, inputs, incoming, packed, kept):
    rows, width = incoming.shape
    hidden = packed[0].shape[0] * PER_ROW
    return pl.pallas_call(
        partial(forward_kernel, moment),
        out_shape=(pltpu.VMEM(incoming.shape, BF16),)
        + tuple(pltpu.VMEM(item.shape, item.dtype) for item in kept),
        in_specs=[SMEM] * 3 + [VMEM] * (4 + len(kept)),
        out_specs=(VMEM,) * (1 + len(kept)),
        input_output_aliases={7 + i: 1 + i for i in range(len(kept))},
        scratch_shapes=[
            pltpu.VMEM((hidden, rows, TILE), F32),
            pltpu.VMEM((hidden // PER_ROW, rows, TILE), BF16),
        ],
        compiler_params=pltpu.CompilerParams(vmem_limit_bytes=LAYER_VMEM),
        cost_estimate=pl.CostEstimate(flops=10**9, bytes_accessed=10**7, transcendentals=0),
        name="layer_forward",
    )(place, upq, dnq, *map(near, (inputs, incoming, *packed, *kept)))


def backward_call(moment, sections, place, upq, dnq, cotangent, incoming, packed, xs, kept):
    rows, width = incoming.shape
    hidden = packed[0].shape[0] * PER_ROW
    return pl.pallas_call(
        partial(backward_kernel, moment, sections),
        out_shape=(pltpu.VMEM(incoming.shape, BF16),)
        + tuple(pltpu.VMEM(item.shape, item.dtype) for item in kept),
        in_specs=[SMEM] * 3 + [VMEM] * (5 + len(kept)),
        out_specs=(VMEM,) * (1 + len(kept)),
        input_output_aliases={8 + i: 1 + i for i in range(len(kept))},
        scratch_shapes=[
            pltpu.VMEM((hidden, rows, TILE), F32),
            pltpu.VMEM((rows, width), F32),
            pltpu.VMEM((rows, width), F32),
        ],
        compiler_params=pltpu.CompilerParams(vmem_limit_bytes=LAYER_VMEM),
        cost_estimate=pl.CostEstimate(flops=10**9, bytes_accessed=10**7, transcendentals=0),
        name="layer_backward",
    )(place, upq, dnq, *map(near, (cotangent, incoming, *packed, xs, *kept)))


def near_call(kernel, name, shapes, scalars, arrays, scratch=(), far=False):
    specs = [SMEM] * len(scalars) + [VMEM] * len(arrays)
    made = jax.ShapeDtypeStruct if far else pltpu.VMEM
    return pl.pallas_call(
        kernel,
        out_shape=tuple(made(*shape) for shape in shapes),
        in_specs=specs,
        out_specs=(VMEM,) * len(shapes),
        scratch_shapes=list(scratch),
        compiler_params=pltpu.CompilerParams(vmem_limit_bytes=SMALL_VMEM),
        name=name,
    )(*scalars, *map(near, arrays))


def dp_send(value, *steps):
    def index(z, y, c):
        return ((z % ALONG) * ALONG + y % ALONG) * CORES + c % CORES

    route = []
    for z in range(ALONG):
        for y in range(ALONG):
            for c in range(CORES):
                dz, dy, dc = steps[c % len(steps)]
                route.append((index(z, y, c), index(z + dz, y + dy, c + dc)))
    return lax.ppermute(value, "dp", route)


def swap_cores(value):
    return dp_send(value, (0, 0, 1))


def along_first(value, d):
    return dp_send(value, (0, d, 0), (d, 0, 0))


def along_second(value, d):
    return dp_send(value, (d, 0, 0), (0, d, 0))


FAR = range(1, ALONG)


def gather(place, mine, other):
    side = mine.shape
    pair = near_call(
        stack_kernel, "pair", [((CORES, *side), BF16)], (), (mine, swap_cores(other))
    )[0]
    pairs = [pair] + [along_first(pair, d) for d in FAR]
    line = near_call(stack_kernel, "line", [((ALONG, CORES, *side), BF16)], (), pairs)[0]
    lines = [line] + [along_second(line, d) for d in FAR]
    others = [swap_cores(piece) for piece in lines]
    full = ((CORES * ALONG * ALONG, *side), BF16)
    return near_call(spread_kernel, "spread", (full, full), (place,), lines + others)


def scatter_sum(place, keep, give):
    side = keep.shape[3:]
    line, pair = ((ALONG, CORES, *side), BF16), ((CORES, *side), BF16)
    came = swap_cores(give)
    lines = near_call(add_cores_kernel, "add_cores", [line] * ALONG, (), (keep, came))
    terms = [lines[0]] + [along_second(lines[d], d) for d in FAR]
    pairs = near_call(add_far_kernel, "add_far", [pair] * ALONG, (), terms)
    terms = [pairs[0]] + [along_first(pairs[d], d) for d in FAR]
    mine, other = near_call(add_last_kernel, "add_last", [(side, F32)] * CORES, (), terms)
    three = (((PER_ROW, TILE, TILE), F32), ((RANK, TILE), F32), ((RANK, MODEL), F32))
    return near_call(
        finish_kernel, "finish", three + three, (place,), (mine, swap_cores(other)), far=True
    )


def buffers(after, *shapes):
    shapes = [(shape, BF16) for shape in shapes]
    return near_call(lambda *refs: None, "buffers", shapes, (), (after,))


def hops(moment, micro, sections, backward):
    first = moment // MOMENT_GROUP * MOMENT_GROUP
    steps = [
        step
        for step in range(sections - 1)
        if any(0 <= first + i - 2 * step < micro for i in range(MOMENT_GROUP))
    ]
    if backward:
        return [(sections - 1 - step, sections - 2 - step) for step in steps]
    return [(step, step + 1) for step in steps]


def per_device(
    inputs, cotangent, up_blocks, up_index, up_left, up_right, down_blocks, down_index,
    down_left, down_right,
):
    sections = lax.axis_size("section")
    micro, rows, width = inputs.shape
    hidden = width // TILE * PER_ROW
    rank = lax.axis_index("dp")
    place = jnp.stack(
        [
            rank // (ALONG * CORES),
            rank // CORES % ALONG,
            rank % CORES,
            lax.axis_index("section"),
        ]
    ).astype(jnp.int32)
    place, upq, dnq = lax.optimization_barrier((place, up_index[0, :, 1], down_index[0, :, 0]))
    side = ((SIDE, TILE), BF16)
    factors = [item[0].T for item in (up_left, up_right, down_left, down_right)]
    packed = gather(
        place,
        *near_call(
            pack_kernel,
            "pack",
            (side, side),
            (place,),
            (up_blocks[0], *factors[:2], down_blocks[0], *factors[2:]),
        ),
    )

    wide, tall, thin = (micro, rows, width), (micro, hidden, rows, TILE), (micro, 2, rows, TILE)
    xs, outs, act, slope, flat, arrived, travelling = buffers(
        packed[0], wide, wide, tall, tall, thin, (rows, width), (rows, width)
    )
    moments = micro + 2 * (sections - 1)
    for moment in range(moments):
        result, xs, outs, act, slope, flat = forward_call(
            moment, place, upq, dnq, inputs, arrived, packed, (xs, outs, act, slope, flat)
        )
        arrived = travelling
        if moment < moments - 2:
            travelling = lax.ppermute(result, "section", hops(moment, micro, sections, False))

    gs, blat, arrived, travelling = buffers(act, wide, thin, (rows, width), (rows, width))
    gp = slope
    for moment in range(moments):
        result, gs, gp, blat = backward_call(
            moment, sections, place, upq, dnq, cotangent, arrived, packed, xs, (gs, gp, blat)
        )
        arrived = travelling
        if moment < moments - 2:
            travelling = lax.ppermute(result, "section", hops(moment, micro, sections, True))

    terms = [
        near_call(
            partial(grads_kernel, keep),
            "grads",
            [((ALONG, ALONG, CORES, SIDE, TILE), BF16)],
            (place, upq, dnq),
            (xs, gs, act, gp, flat, blat),
            (pltpu.VMEM(wide, BF16),),
        )[0]
        for keep in (False, True)
    ]
    up_grad, up_left_grad, up_right_grad, down_grad, down_right_grad, down_left_grad = scatter_sum(
        place, terms[1], terms[0]
    )
    return (
        outs[None],
        up_grad[None],
        up_left_grad.T[None],
        up_right_grad.T[None],
        down_grad[None],
        down_left_grad.T[None],
        down_right_grad.T[None],
    )


def solution(mesh):
    in_specs = (
        P(None, "dp", None),
        P(None, "dp", None),
        P("section", "dp", None, None),
        P("section", None, None),
        P("section", "dp", None),
        P("section", "dp", None),
        P("section", "dp", None, None),
        P("section", None, None),
        P("section", "dp", None),
        P("section", "dp", None),
    )
    out_specs = (
        P("section", None, "dp", None),
        P("section", "dp", None, None),
        P("section", "dp", None),
        P("section", "dp", None),
        P("section", "dp", None, None),
        P("section", "dp", None),
        P("section", "dp", None),
    )
    return jax.shard_map(
        per_device, mesh=mesh, in_specs=in_specs, out_specs=out_specs, check_vma=False
    )
```

```python
import math
from functools import partial

import jax
import jax.numpy as jnp
from jax import lax
from jax.experimental import pallas as pl
from jax.experimental.pallas import tpu as pltpu
from jax.sharding import Mesh
from jax.sharding import PartitionSpec as P

NORM_EPS = 1e-05
GELU_CUBIC = 0.044715
GELU_ROOT = math.sqrt(2.0 / math.pi)

TILE = 128
PER_ROW = 4
RANK = 16
MODEL = PER_ROW * TILE
HIDDEN = MODEL + RANK
SIDE = HIDDEN + PER_ROW * RANK
UP = 0
DOWN = 1
ALONG = 4
CORES = 2
Z_SECTIONS = 4
SMALL_VMEM = 12 * 1024 * 1024
UNROLL = 16
MOMENT_GROUP = 4
LAYER_VMEM = 12 * 1024 * 1024
F32 = jnp.float32
BF16 = jnp.bfloat16


def mm(left, right):
    return lax.dot_general(left, right, (((1,), (0,)), ((), ())), preferred_element_type=F32)


def mm_nt(left, right):
    return lax.dot_general(left, right, (((1,), (1,)), ((), ())), preferred_element_type=F32)


def mm_tn(left, right):
    return lax.dot_general(left, right, (((0,), (0,)), ((), ())), preferred_element_type=F32)


def lanes(pieces):
    return jnp.concatenate(pieces, axis=1)


def low_rows(side, index):
    return lanes(
        [side[index, HIDDEN + RANK * i : HIDDEN + RANK * (i + 1), :] for i in range(PER_ROW)]
    )


def normalised(x_ref):
    xf = x_ref[...].astype(F32)
    scaling = lax.rsqrt(jnp.mean(xf * xf, axis=-1, keepdims=True) + NORM_EPS)
    return xf, scaling


def slot_at(number, micro):
    live = (number >= 0) & (number < micro)
    return live, jnp.clip(number, 0, micro - 1)


def forward_kernel(
    moment, place, upq, dnq, inputs, incoming, wu, wd, xs_in, outs_in, act_in, slope_in, lat_in,
    y, xs, outs, act, slope, lat,
    pre, nv,
):
    position = place[3]
    live, slot = slot_at(moment - 2 * position, inputs.shape[0])
    blocks = wu.shape[0]
    hidden = pre.shape[0]
    rows = y.shape[0]

    @pl.when(live)
    def _():
        @pl.when(position == 0)
        def _():
            xs[slot] = inputs[slot]

        @pl.when(position != 0)
        def _():
            xs[slot] = incoming[...]

        xf, scaling = normalised(xs.at[slot])
        normed = (xf * scaling).astype(BF16)
        for p in range(blocks):
            nv[p] = normed[:, p * TILE : (p + 1) * TILE]

        def to_latent(j, total):
            pair = lanes([nv[2 * j], nv[2 * j + 1]])
            factor = lanes([wu[2 * j + i, MODEL:HIDDEN, :] for i in range(2)])
            return total + mm_nt(pair, factor)

        none = jnp.zeros((rows, RANK), F32)
        up_latent = lax.fori_loop(0, blocks // 2, to_latent, none, unroll=UNROLL // 2).astype(BF16)
        lat[slot, 0, :, 0:RANK] = up_latent

        def low_rank(p, carry):
            low = mm(up_latent, low_rows(wu, p))
            for i in range(PER_ROW):
                pre[PER_ROW * p + i] = low[:, i * TILE : (i + 1) * TILE]
            return carry

        lax.fori_loop(0, blocks, low_rank, 0, unroll=UNROLL)

        def up_blocks(p, carry):
            product = mm(nv[p], lanes([wu[p, i * TILE : (i + 1) * TILE, :] for i in range(PER_ROW)]))
            where = [upq[PER_ROW * p + i] for i in range(PER_ROW)]
            sums = [pre[q] + product[:, i * TILE : (i + 1) * TILE] for i, q in enumerate(where)]
            for q, value in zip(where, sums):
                pre[q] = value
            return carry

        lax.fori_loop(0, blocks, up_blocks, 0, unroll=UNROLL)

        def gelu(q, carry):
            u = pre[q]
            square = u * u
            bend = jnp.tanh(u * (GELU_ROOT + GELU_ROOT * GELU_CUBIC * square))
            half = 0.5 + 0.5 * bend
            act[slot, q] = (u * half).astype(BF16)
            inner = 0.5 * GELU_ROOT + 1.5 * GELU_ROOT * GELU_CUBIC * square
            slopes = half + (u * inner) * (1.0 - bend * bend)
            slope[slot, q] = slopes.astype(BF16)
            return carry

        lax.fori_loop(0, hidden, gelu, 0, unroll=8)

        def from_hidden(p, total):
            return total + mm_nt(
                lanes([act[slot, PER_ROW * p + i] for i in range(PER_ROW)]), low_rows(wd, p)
            )

        down_latent = lax.fori_loop(0, blocks, from_hidden, none, unroll=UNROLL).astype(BF16)
        lat[slot, 1, :, 0:RANK] = down_latent

        def down_blocks(p, carry):
            left = lanes([act[slot, dnq[PER_ROW * p + i]] for i in range(PER_ROW)])
            product = mm(left, wd[p, 0:MODEL, :])
            product += mm(down_latent, wd[p, MODEL:HIDDEN, :])
            cols = pl.ds(pl.multiple_of(p * TILE, TILE), TILE)
            result = (xs[slot, :, cols].astype(F32) + product).astype(BF16)
            y[:, cols] = result
            outs[slot, :, cols] = result
            return carry

        lax.fori_loop(0, blocks, down_blocks, 0, unroll=UNROLL)


def backward_kernel(
    moment, sections, place, upq, dnq, cotangent, incoming, wu, wd, xs, gs_in, slope, lat_in,
    y, gs, gp, lat,
    ga, norm, unit,
):
    position = place[3]
    live, slot = slot_at(moment - 2 * (sections - 1 - position), cotangent.shape[0])
    blocks = wu.shape[0]
    hidden = ga.shape[0]
    rows = y.shape[0]

    @pl.when(live)
    def _():
        @pl.when(position == sections - 1)
        def _():
            gs[slot] = cotangent[slot]

        @pl.when(position != sections - 1)
        def _():
            gs[slot] = incoming[...]

        def columns(p, count=1):
            return pl.ds(pl.multiple_of(p * TILE, TILE), count * TILE)

        def to_latent(j, total):
            factor = lanes([wd[2 * j + i, MODEL:HIDDEN, :] for i in range(2)])
            return total + mm_nt(gs[slot, :, columns(2 * j, 2)], factor)

        none = jnp.zeros((rows, RANK), F32)
        down = lax.fori_loop(0, blocks // 2, to_latent, none, unroll=UNROLL // 2).astype(BF16)
        lat[slot, 1, :, 0:RANK] = down

        def low_rank(p, carry):
            low = mm(down, low_rows(wd, p))
            for i in range(PER_ROW):
                ga[PER_ROW * p + i] = low[:, i * TILE : (i + 1) * TILE]
            return carry

        lax.fori_loop(0, blocks, low_rank, 0, unroll=UNROLL)

        def down_blocks(p, carry):
            product = mm_nt(gs[slot, :, columns(p)], wd[p, 0:MODEL, :])
            where = [dnq[PER_ROW * p + i] for i in range(PER_ROW)]
            sums = [ga[q] + product[:, i * TILE : (i + 1) * TILE] for i, q in enumerate(where)]
            for q, value in zip(where, sums):
                ga[q] = value
            return carry

        lax.fori_loop(0, blocks, down_blocks, 0, unroll=UNROLL)

        def slopes(q, carry):
            gp[slot, q] = (ga[q] * slope[slot, q].astype(F32)).astype(BF16)
            return carry

        lax.fori_loop(0, hidden, slopes, 0, unroll=8)

        def from_hidden(p, total):
            return total + mm_nt(
                lanes([gp[slot, PER_ROW * p + i] for i in range(PER_ROW)]), low_rows(wu, p)
            )

        up = lax.fori_loop(0, blocks, from_hidden, none, unroll=UNROLL).astype(BF16)
        lat[slot, 0, :, 0:RANK] = up
        xf, scaling = normalised(xs.at[slot])
        unit[...] = xf * scaling

        def up_blocks(p, along):
            left = lanes([gp[slot, upq[PER_ROW * p + i]] for i in range(PER_ROW)])
            piece = lanes([wu[p, i * TILE : (i + 1) * TILE, :] for i in range(PER_ROW)])
            product = mm_nt(left, piece)
            product += mm(up, wu[p, MODEL:HIDDEN, :])
            norm[:, columns(p)] = product
            return along + product * unit[:, columns(p)]

        along = jnp.zeros((rows, TILE), F32)
        along = lax.fori_loop(0, blocks, up_blocks, along, unroll=UNROLL)
        mean = jnp.sum(along, axis=-1, keepdims=True) * (1.0 / (blocks * TILE))
        y[...] = (
            gs[slot].astype(F32) + scaling * (norm[...] - unit[...] * mean)
        ).astype(BF16)


def far_along_z(place, side):
    return jnp.logical_and(side == UP, place[3] < Z_SECTIONS)


def place_of(place, p, side):
    dz = lax.rem(p // (ALONG * CORES) - place[0] + ALONG, ALONG)
    dy = lax.rem(lax.rem(p // CORES, ALONG) - place[1] + ALONG, ALONG)
    other = lax.rem(lax.rem(p, CORES) + side, CORES)
    long_z = far_along_z(place, side)
    return jnp.where(long_z, dz, dy), jnp.where(long_z, dy, dz), other


def column(ref, p):
    tokens = ref.shape[0] * ref.shape[1]
    return ref[:, :, pl.ds(pl.multiple_of(p * TILE, TILE), TILE)].reshape(tokens, TILE)


def of_hidden(ref, q):
    return ref[:, pl.ds(q, 1)].reshape(ref.shape[0] * ref.shape[2], TILE)


def latent(ref, kind):
    return ref[:, kind, :, 0:RANK].reshape(ref.shape[0] * ref.shape[2], RANK)


def put_low(out, where, low):
    for i in range(PER_ROW):
        rows = slice(HIDDEN + RANK * i, HIDDEN + RANK * (i + 1))
        out[(*where, rows, slice(None))] = low[:, i * TILE : (i + 1) * TILE].astype(BF16)


def down_grads(place, dnq, gs, act, flat, blat, out):
    blocks = gs.shape[2] // TILE
    down_latent, grad_down_latent = latent(flat, 1), latent(blat, 1)

    def one(p, carry):
        where = place_of(place, p, DOWN)
        g = column(gs, p)
        for i in range(PER_ROW):
            product = mm_tn(of_hidden(act, dnq[PER_ROW * p + i]), g)
            out[(*where, slice(i * TILE, (i + 1) * TILE), slice(None))] = product.astype(BF16)
        out[(*where, slice(MODEL, HIDDEN), slice(None))] = mm_tn(down_latent, g).astype(BF16)
        here = lanes([of_hidden(act, PER_ROW * p + i) for i in range(PER_ROW)])
        put_low(out, where, mm_tn(grad_down_latent, here))
        return carry

    lax.fori_loop(0, blocks, one, 0, unroll=2)


def up_grads(place, upq, xs, gp, flat, blat, out, normed):
    blocks = xs.shape[2] // TILE
    xf, scaling = normalised(xs)
    normed[...] = (xf * scaling).astype(BF16)
    up_latent, grad_up_latent = latent(flat, 0), latent(blat, 0)

    def one(p, carry):
        where = place_of(place, p, UP)
        n = column(normed, p)
        there = lanes([of_hidden(gp, upq[PER_ROW * p + i]) for i in range(PER_ROW)])
        product = mm_tn(n, there)
        for i in range(PER_ROW):
            out[(*where, slice(i * TILE, (i + 1) * TILE), slice(None))] = product[
                :, i * TILE : (i + 1) * TILE
            ].astype(BF16)
        out[(*where, slice(MODEL, HIDDEN), slice(None))] = mm_tn(grad_up_latent, n).astype(BF16)
        here = lanes([of_hidden(gp, PER_ROW * p + i) for i in range(PER_ROW)])
        put_low(out, where, mm_tn(up_latent, here))
        return carry

    lax.fori_loop(0, blocks, one, 0, unroll=2)


def grads_kernel(keep, place, upq, dnq, xs, gs, act, gp, flat, blat, out, normed):
    core = place[2]

    @pl.when(core == (UP if keep else DOWN))
    def _():
        up_grads(place, upq, xs, gp, flat, blat, out, normed)

    @pl.when(core == (DOWN if keep else UP))
    def _():
        down_grads(place, dnq, gs, act, flat, blat, out)


def pack_kernel(
    place, up_blocks, up_left, up_right, down_blocks, down_left, down_right, inputs, cotangent,
    mine, other, near_inputs, near_cotangent, sem,
):
    def copies(up, down):
        pairs = [(inputs, near_inputs), (cotangent, near_cotangent)]
        for out, tiles, model, hidden in (
            (up, up_blocks, up_left, up_right),
            (down, down_blocks, down_right, down_left),
        ):
            pairs.append((model, out.at[MODEL:HIDDEN, :]))
            for i in range(PER_ROW):
                rows = slice(HIDDEN + RANK * i, HIDDEN + RANK * (i + 1))
                cols = slice(i * TILE, (i + 1) * TILE)
                pairs.append((tiles.at[i], out.at[cols, :]))
                pairs.append((hidden.at[:, cols], out.at[rows, :]))
        made = [pltpu.make_async_copy(*pair, sem.at[i]) for i, pair in enumerate(pairs)]
        for copy in made[2:] + made[:2]:
            copy.start()
        for copy in made:
            copy.wait()

    @pl.when(place[2] == UP)
    def _():
        copies(mine, other)

    @pl.when(place[2] == DOWN)
    def _():
        copies(other, mine)


def stack_kernel(*refs):
    for d, piece in enumerate(refs[:-1]):
        refs[-1][d] = piece[...]


def spread_kernel(place, *refs):
    mine, other, sides = refs[:ALONG], refs[ALONG : 2 * ALONG], refs[2 * ALONG :]
    z, y, core = place[0], place[1], place[2]
    for side, out in zip((UP, DOWN), sides):
        long_z = far_along_z(place, side)
        for pieces, holder in ((mine, side), (other, 1 - side)):

            @pl.when(core == holder)
            def _():
                for outer in range(ALONG):
                    for inner in range(ALONG):
                        dz = jnp.where(long_z, outer, inner)
                        dy = outer + inner - dz
                        back_z = lax.rem(z - dz + ALONG, ALONG)
                        back_y = lax.rem(y - dy + ALONG, ALONG)
                        chip = back_z * ALONG + back_y
                        for far in range(CORES):
                            out[chip * CORES + (side + far) % CORES] = pieces[outer][inner, far]


def add_cores_kernel(mine, came, *outs):
    for outer, out in enumerate(outs):
        for inner in range(ALONG):
            total = mine[outer, inner].astype(F32) + came[outer, inner].astype(F32)
            out[inner] = total.astype(BF16)


def add_far_kernel(*refs):
    terms, outs = refs[:ALONG], refs[ALONG:]
    for inner, out in enumerate(outs):
        total = terms[0][inner].astype(F32)
        for came in terms[1:]:
            total += came[inner].astype(F32)
        out[...] = total.astype(BF16)


def add_last_kernel(*refs):
    terms, outs = refs[:ALONG], refs[ALONG:]
    for far, out in enumerate(outs):
        total = terms[0][far].astype(F32)
        for came in terms[1:]:
            total += came[far].astype(F32)
        out[...] = total


def finish_kernel(place, mine, other, *outs):
    for side, (tiles, model, hidden) in ((UP, outs[:3]), (DOWN, outs[3:])):
        for total, core in ((mine, side), (other, 1 - side)):

            @pl.when(place[2] == core)
            def _():
                for i in range(PER_ROW):
                    tiles[i] = total[i * TILE : (i + 1) * TILE, :]
                model[...] = total[MODEL:HIDDEN, :]
                for i in range(PER_ROW):
                    rows = slice(HIDDEN + RANK * i, HIDDEN + RANK * (i + 1))
                    hidden[:, i * TILE : (i + 1) * TILE] = total[rows, :]


SMEM = pl.BlockSpec(memory_space=pltpu.SMEM)
VMEM = pl.BlockSpec(memory_space=pltpu.VMEM)
HBM = pl.BlockSpec(memory_space=pl.ANY)


def near(array):
    return pltpu.with_memory_space_constraint(array, pltpu.VMEM)


def forward_call(moment, place, upq, dnq, inputs, incoming, packed, kept):
    rows, width = incoming.shape
    hidden = packed[0].shape[0] * PER_ROW
    return pl.pallas_call(
        partial(forward_kernel, moment),
        out_shape=(pltpu.VMEM(incoming.shape, BF16),)
        + tuple(pltpu.VMEM(item.shape, item.dtype) for item in kept),
        in_specs=[SMEM] * 3 + [VMEM] * (4 + len(kept)),
        out_specs=(VMEM,) * (1 + len(kept)),
        input_output_aliases={7 + i: 1 + i for i in range(len(kept))},
        scratch_shapes=[
            pltpu.VMEM((hidden, rows, TILE), F32),
            pltpu.VMEM((hidden // PER_ROW, rows, TILE), BF16),
        ],
        compiler_params=pltpu.CompilerParams(vmem_limit_bytes=LAYER_VMEM),
        cost_estimate=pl.CostEstimate(flops=10**9, bytes_accessed=10**7, transcendentals=0),
        name="layer_forward",
    )(place, upq, dnq, *map(near, (inputs, incoming, *packed, *kept)))


def backward_call(moment, sections, place, upq, dnq, cotangent, incoming, packed, xs, kept):
    rows, width = incoming.shape
    hidden = packed[0].shape[0] * PER_ROW
    return pl.pallas_call(
        partial(backward_kernel, moment, sections),
        out_shape=(pltpu.VMEM(incoming.shape, BF16),)
        + tuple(pltpu.VMEM(item.shape, item.dtype) for item in kept),
        in_specs=[SMEM] * 3 + [VMEM] * (5 + len(kept)),
        out_specs=(VMEM,) * (1 + len(kept)),
        input_output_aliases={8 + i: 1 + i for i in range(len(kept))},
        scratch_shapes=[
            pltpu.VMEM((hidden, rows, TILE), F32),
            pltpu.VMEM((rows, width), F32),
            pltpu.VMEM((rows, width), F32),
        ],
        compiler_params=pltpu.CompilerParams(vmem_limit_bytes=LAYER_VMEM),
        cost_estimate=pl.CostEstimate(flops=10**9, bytes_accessed=10**7, transcendentals=0),
        name="layer_backward",
    )(place, upq, dnq, *map(near, (cotangent, incoming, *packed, xs, *kept)))


def near_call(kernel, name, shapes, scalars, arrays, scratch=(), far=False):
    specs = [SMEM] * len(scalars) + [VMEM] * len(arrays)
    made = jax.ShapeDtypeStruct if far else pltpu.VMEM
    return pl.pallas_call(
        kernel,
        out_shape=tuple(made(*shape) for shape in shapes),
        in_specs=specs,
        out_specs=(VMEM,) * len(shapes),
        scratch_shapes=list(scratch),
        compiler_params=pltpu.CompilerParams(vmem_limit_bytes=SMALL_VMEM),
        name=name,
    )(*scalars, *map(near, arrays))


def send(value, step):
    sections = lax.axis_size("section")

    def index(section, z, y, c):
        return ((section * ALONG + z % ALONG) * ALONG + y % ALONG) * CORES + c % CORES

    route = []
    for section in range(sections):
        for z in range(ALONG):
            for y in range(ALONG):
                for c in range(CORES):
                    dz, dy, dc = step(section, c)
                    target = index(section, z + dz, y + dy, c + dc)
                    route.append((index(section, z, y, c), target))
    return lax.ppermute(value, ("section", "dp"), route)


def swap_cores(value):
    return send(value, lambda section, core: (0, 0, 1))


def along_first(value, d):
    return send(
        value,
        lambda section, core: (0, d, 0) if core == UP and section < Z_SECTIONS else (d, 0, 0),
    )


def along_second(value, d):
    return send(
        value,
        lambda section, core: (d, 0, 0) if core == UP and section < Z_SECTIONS else (0, d, 0),
    )


FAR = range(1, ALONG)


def gather(place, mine, other):
    side = mine.shape
    pair = near_call(
        stack_kernel, "pair", [((CORES, *side), BF16)], (), (mine, swap_cores(other))
    )[0]
    pairs = [pair] + [along_first(pair, d) for d in FAR]
    line = near_call(stack_kernel, "line", [((ALONG, CORES, *side), BF16)], (), pairs)[0]
    lines = [line] + [along_second(line, d) for d in FAR]
    others = [swap_cores(piece) for piece in lines]
    full = ((CORES * ALONG * ALONG, *side), BF16)
    return near_call(spread_kernel, "spread", (full, full), (place,), lines + others)


def scatter_sum(place, keep, give):
    side = keep.shape[3:]
    line, pair = ((ALONG, CORES, *side), BF16), ((CORES, *side), BF16)
    came = swap_cores(give)
    lines = near_call(add_cores_kernel, "add_cores", [line] * ALONG, (), (keep, came))
    terms = [lines[0]] + [along_second(lines[d], d) for d in FAR]
    pairs = near_call(add_far_kernel, "add_far", [pair] * ALONG, (), terms)
    terms = [pairs[0]] + [along_first(pairs[d], d) for d in FAR]
    mine, other = near_call(add_last_kernel, "add_last", [(side, F32)] * CORES, (), terms)
    three = (((PER_ROW, TILE, TILE), F32), ((RANK, TILE), F32), ((RANK, MODEL), F32))
    return near_call(
        finish_kernel, "finish", three + three, (place,), (mine, swap_cores(other)), far=True
    )


def buffers(after, *shapes):
    shapes = [(shape, BF16) for shape in shapes]
    return near_call(lambda *refs: None, "buffers", shapes, (), (after,))


def hops(moment, micro, sections, backward):
    first = moment // MOMENT_GROUP * MOMENT_GROUP
    steps = [
        step
        for step in range(sections - 1)
        if any(0 <= first + i - 2 * step < micro for i in range(MOMENT_GROUP))
    ]
    if backward:
        return [(sections - 1 - step, sections - 2 - step) for step in steps]
    return [(step, step + 1) for step in steps]


def per_device(
    inputs, cotangent, up_blocks, up_index, up_left, up_right, down_blocks, down_index,
    down_left, down_right,
):
    sections = lax.axis_size("section")
    micro, rows, width = inputs.shape
    hidden = width // TILE * PER_ROW
    rank = lax.axis_index("dp")
    place = jnp.stack(
        [
            rank // (ALONG * CORES),
            rank // CORES % ALONG,
            rank % CORES,
            lax.axis_index("section"),
        ]
    ).astype(jnp.int32)
    place, upq, dnq = lax.optimization_barrier((place, up_index[0, :, 1], down_index[0, :, 0]))
    side = ((SIDE, TILE), BF16)
    factors = [item[0].T for item in (up_left, up_right, down_left, down_right)]
    near_tokens = (inputs.shape, BF16)
    mine, other, inputs, cotangent = pl.pallas_call(
        pack_kernel,
        out_shape=tuple(pltpu.VMEM(*shape) for shape in (side, side, near_tokens, near_tokens)),
        in_specs=[SMEM] + [HBM] * 8,
        out_specs=(VMEM,) * 4,
        scratch_shapes=[pltpu.SemaphoreType.DMA((2 + 2 * (1 + 2 * PER_ROW),))],
        compiler_params=pltpu.CompilerParams(vmem_limit_bytes=SMALL_VMEM),
        name="pack",
    )(place, up_blocks[0], *factors[:2], down_blocks[0], *factors[2:], inputs, cotangent)
    packed = gather(place, mine, other)

    wide, tall, thin = (micro, rows, width), (micro, hidden, rows, TILE), (micro, 2, rows, TILE)
    xs, outs, act, slope, flat, arrived, travelling = buffers(
        packed[0], wide, wide, tall, tall, thin, (rows, width), (rows, width)
    )
    moments = micro + 2 * (sections - 1)
    for moment in range(moments):
        result, xs, outs, act, slope, flat = forward_call(
            moment, place, upq, dnq, inputs, arrived, packed, (xs, outs, act, slope, flat)
        )
        arrived = travelling
        if moment < moments - 2:
            travelling = lax.ppermute(result, "section", hops(moment, micro, sections, False))

    gs, blat, arrived, travelling = buffers(act, wide, thin, (rows, width), (rows, width))
    gp = slope
    for moment in range(moments):
        result, gs, gp, blat = backward_call(
            moment, sections, place, upq, dnq, cotangent, arrived, packed, xs, (gs, gp, blat)
        )
        arrived = travelling
        if moment < moments - 2:
            travelling = lax.ppermute(result, "section", hops(moment, micro, sections, True))

    terms = [
        near_call(
            partial(grads_kernel, keep),
            "grads",
            [((ALONG, ALONG, CORES, SIDE, TILE), BF16)],
            (place, upq, dnq),
            (xs, gs, act, gp, flat, blat),
            (pltpu.VMEM(wide, BF16),),
        )[0]
        for keep in (False, True)
    ]
    up_grad, up_left_grad, up_right_grad, down_grad, down_right_grad, down_left_grad = scatter_sum(
        place, terms[1], terms[0]
    )
    return (
        outs[None],
        up_grad[None],
        up_left_grad.T[None],
        up_right_grad.T[None],
        down_grad[None],
        down_left_grad.T[None],
        down_right_grad.T[None],
    )


def solution(mesh):
    in_specs = (
        P(None, "dp", None),
        P(None, "dp", None),
        P("section", "dp", None, None),
        P("section", None, None),
        P("section", "dp", None),
        P("section", "dp", None),
        P("section", "dp", None, None),
        P("section", None, None),
        P("section", "dp", None),
        P("section", "dp", None),
    )
    out_specs = (
        P("section", None, "dp", None),
        P("section", "dp", None, None),
        P("section", "dp", None),
        P("section", "dp", None),
        P("section", "dp", None, None),
        P("section", "dp", None),
        P("section", "dp", None),
    )
    return jax.shard_map(
        per_device, mesh=mesh, in_specs=in_specs, out_specs=out_specs, check_vma=False
    )
```

```python
import math
from functools import partial

import jax
import jax.numpy as jnp
from jax import lax
from jax.experimental import pallas as pl
from jax.experimental.pallas import tpu as pltpu
from jax.sharding import Mesh
from jax.sharding import PartitionSpec as P

NORM_EPS = 1e-05
GELU_CUBIC = 0.044715
GELU_ROOT = math.sqrt(2.0 / math.pi)

TILE = 128
PER_ROW = 4
RANK = 16
MODEL = PER_ROW * TILE
HIDDEN = MODEL + RANK
SIDE = HIDDEN + PER_ROW * RANK
UP = 0
DOWN = 1
ALONG = 4
CORES = 2
Z_SECTIONS = 4
SMALL_VMEM = 12 * 1024 * 1024
UNROLL = 16
MOMENT_GROUP = 4
LAYER_VMEM = 12 * 1024 * 1024
F32 = jnp.float32
BF16 = jnp.bfloat16


def mm(left, right):
    return lax.dot_general(left, right, (((1,), (0,)), ((), ())), preferred_element_type=F32)


def mm_nt(left, right):
    return lax.dot_general(left, right, (((1,), (1,)), ((), ())), preferred_element_type=F32)


def mm_tn(left, right):
    return lax.dot_general(left, right, (((0,), (0,)), ((), ())), preferred_element_type=F32)


def lanes(pieces):
    return jnp.concatenate(pieces, axis=1)


def low_rows(side, index):
    return lanes(
        [side[index, HIDDEN + RANK * i : HIDDEN + RANK * (i + 1), :] for i in range(PER_ROW)]
    )


def normalised(x_ref):
    xf = x_ref[...].astype(F32)
    scaling = lax.rsqrt(jnp.mean(xf * xf, axis=-1, keepdims=True) + NORM_EPS)
    return xf, scaling


def slot_at(number, micro):
    live = (number >= 0) & (number < micro)
    return live, jnp.clip(number, 0, micro - 1)


def forward_kernel(
    moment, place, upq, dnq, inputs, incoming, wu, wd, xs_in, outs_in, act_in, slope_in, lat_in,
    y, xs, outs, act, slope, lat,
    pre, nv,
):
    position = place[3]
    live, slot = slot_at(moment - 2 * position, inputs.shape[0])
    blocks = wu.shape[0]
    hidden = pre.shape[0]
    rows = y.shape[0]

    @pl.when(live)
    def _():
        @pl.when(position == 0)
        def _():
            xs[slot] = inputs[slot]

        @pl.when(position != 0)
        def _():
            xs[slot] = incoming[...]

        xf, scaling = normalised(xs.at[slot])
        normed = (xf * scaling).astype(BF16)
        for p in range(blocks):
            nv[p] = normed[:, p * TILE : (p + 1) * TILE]

        def to_latent(j, total):
            pair = lanes([nv[2 * j], nv[2 * j + 1]])
            factor = lanes([wu[2 * j + i, MODEL:HIDDEN, :] for i in range(2)])
            return total + mm_nt(pair, factor)

        none = jnp.zeros((rows, RANK), F32)
        up_latent = lax.fori_loop(0, blocks // 2, to_latent, none, unroll=UNROLL // 2).astype(BF16)
        lat[slot, 0, :, 0:RANK] = up_latent

        def low_rank(p, carry):
            low = mm(up_latent, low_rows(wu, p))
            for i in range(PER_ROW):
                pre[PER_ROW * p + i] = low[:, i * TILE : (i + 1) * TILE]
            return carry

        lax.fori_loop(0, blocks, low_rank, 0, unroll=UNROLL)

        def up_blocks(p, carry):
            product = mm(nv[p], lanes([wu[p, i * TILE : (i + 1) * TILE, :] for i in range(PER_ROW)]))
            where = [upq[PER_ROW * p + i] for i in range(PER_ROW)]
            sums = [pre[q] + product[:, i * TILE : (i + 1) * TILE] for i, q in enumerate(where)]
            for q, value in zip(where, sums):
                pre[q] = value
            return carry

        lax.fori_loop(0, blocks, up_blocks, 0, unroll=UNROLL)

        def gelu(q, carry):
            u = pre[q]
            square = u * u
            bend = jnp.tanh(u * (GELU_ROOT + GELU_ROOT * GELU_CUBIC * square))
            half = 0.5 + 0.5 * bend
            act[slot, q] = (u * half).astype(BF16)
            inner = 0.5 * GELU_ROOT + 1.5 * GELU_ROOT * GELU_CUBIC * square
            slopes = half + (u * inner) * (1.0 - bend * bend)
            slope[slot, q] = slopes.astype(BF16)
            return carry

        lax.fori_loop(0, hidden, gelu, 0, unroll=8)

        def from_hidden(p, total):
            return total + mm_nt(
                lanes([act[slot, PER_ROW * p + i] for i in range(PER_ROW)]), low_rows(wd, p)
            )

        down_latent = lax.fori_loop(0, blocks, from_hidden, none, unroll=UNROLL).astype(BF16)
        lat[slot, 1, :, 0:RANK] = down_latent

        def down_blocks(p, carry):
            left = lanes([act[slot, dnq[PER_ROW * p + i]] for i in range(PER_ROW)])
            product = mm(left, wd[p, 0:MODEL, :])
            product += mm(down_latent, wd[p, MODEL:HIDDEN, :])
            cols = pl.ds(pl.multiple_of(p * TILE, TILE), TILE)
            result = (xs[slot, :, cols].astype(F32) + product).astype(BF16)
            y[:, cols] = result
            outs[slot, :, cols] = result
            return carry

        lax.fori_loop(0, blocks, down_blocks, 0, unroll=UNROLL)


def backward_kernel(
    moment, sections, place, upq, dnq, cotangent, incoming, wu, wd, xs, gs_in, slope, lat_in,
    y, gs, gp, lat,
    ga, norm, unit,
):
    position = place[3]
    live, slot = slot_at(moment - 2 * (sections - 1 - position), cotangent.shape[0])
    blocks = wu.shape[0]
    hidden = ga.shape[0]
    rows = y.shape[0]

    @pl.when(live)
    def _():
        @pl.when(position == sections - 1)
        def _():
            gs[slot] = cotangent[slot]

        @pl.when(position != sections - 1)
        def _():
            gs[slot] = incoming[...]

        def columns(p, count=1):
            return pl.ds(pl.multiple_of(p * TILE, TILE), count * TILE)

        def to_latent(j, total):
            factor = lanes([wd[2 * j + i, MODEL:HIDDEN, :] for i in range(2)])
            return total + mm_nt(gs[slot, :, columns(2 * j, 2)], factor)

        none = jnp.zeros((rows, RANK), F32)
        down = lax.fori_loop(0, blocks // 2, to_latent, none, unroll=UNROLL // 2).astype(BF16)
        lat[slot, 1, :, 0:RANK] = down

        def low_rank(p, carry):
            low = mm(down, low_rows(wd, p))
            for i in range(PER_ROW):
                ga[PER_ROW * p + i] = low[:, i * TILE : (i + 1) * TILE]
            return carry

        lax.fori_loop(0, blocks, low_rank, 0, unroll=UNROLL)

        def down_blocks(p, carry):
            product = mm_nt(gs[slot, :, columns(p)], wd[p, 0:MODEL, :])
            where = [dnq[PER_ROW * p + i] for i in range(PER_ROW)]
            sums = [ga[q] + product[:, i * TILE : (i + 1) * TILE] for i, q in enumerate(where)]
            for q, value in zip(where, sums):
                ga[q] = value
            return carry

        lax.fori_loop(0, blocks, down_blocks, 0, unroll=UNROLL)

        def slopes(q, carry):
            gp[slot, q] = (ga[q] * slope[slot, q].astype(F32)).astype(BF16)
            return carry

        lax.fori_loop(0, hidden, slopes, 0, unroll=8)

        def from_hidden(p, total):
            return total + mm_nt(
                lanes([gp[slot, PER_ROW * p + i] for i in range(PER_ROW)]), low_rows(wu, p)
            )

        up = lax.fori_loop(0, blocks, from_hidden, none, unroll=UNROLL).astype(BF16)
        lat[slot, 0, :, 0:RANK] = up
        xf, scaling = normalised(xs.at[slot])
        unit[...] = xf * scaling

        def up_blocks(p, along):
            left = lanes([gp[slot, upq[PER_ROW * p + i]] for i in range(PER_ROW)])
            piece = lanes([wu[p, i * TILE : (i + 1) * TILE, :] for i in range(PER_ROW)])
            product = mm_nt(left, piece)
            product += mm(up, wu[p, MODEL:HIDDEN, :])
            norm[:, columns(p)] = product
            return along + product * unit[:, columns(p)]

        along = jnp.zeros((rows, TILE), F32)
        along = lax.fori_loop(0, blocks, up_blocks, along, unroll=UNROLL)
        mean = jnp.sum(along, axis=-1, keepdims=True) * (1.0 / (blocks * TILE))
        y[...] = (
            gs[slot].astype(F32) + scaling * (norm[...] - unit[...] * mean)
        ).astype(BF16)


def far_along_z(place, side):
    return jnp.logical_and(side == UP, place[3] < Z_SECTIONS)


def place_of(place, p, side):
    dz = lax.rem(p // (ALONG * CORES) - place[0] + ALONG, ALONG)
    dy = lax.rem(lax.rem(p // CORES, ALONG) - place[1] + ALONG, ALONG)
    other = lax.rem(lax.rem(p, CORES) + side, CORES)
    long_z = far_along_z(place, side)
    return jnp.where(long_z, dz, dy), jnp.where(long_z, dy, dz), other


def column(ref, p):
    tokens = ref.shape[0] * ref.shape[1]
    return ref[:, :, pl.ds(pl.multiple_of(p * TILE, TILE), TILE)].reshape(tokens, TILE)


def of_hidden(ref, q):
    return ref[:, pl.ds(q, 1)].reshape(ref.shape[0] * ref.shape[2], TILE)


def latent(ref, kind):
    return ref[:, kind, :, 0:RANK].reshape(ref.shape[0] * ref.shape[2], RANK)


def put_low(out, where, low):
    for i in range(PER_ROW):
        rows = slice(HIDDEN + RANK * i, HIDDEN + RANK * (i + 1))
        out[(*where, rows, slice(None))] = low[:, i * TILE : (i + 1) * TILE].astype(BF16)


def down_grads(place, dnq, gs, act, flat, blat, out):
    blocks = gs.shape[2] // TILE
    down_latent, grad_down_latent = latent(flat, 1), latent(blat, 1)

    def one(p, carry):
        where = place_of(place, p, DOWN)
        g = column(gs, p)
        for i in range(PER_ROW):
            product = mm_tn(of_hidden(act, dnq[PER_ROW * p + i]), g)
            out[(*where, slice(i * TILE, (i + 1) * TILE), slice(None))] = product.astype(BF16)
        out[(*where, slice(MODEL, HIDDEN), slice(None))] = mm_tn(down_latent, g).astype(BF16)
        here = lanes([of_hidden(act, PER_ROW * p + i) for i in range(PER_ROW)])
        put_low(out, where, mm_tn(grad_down_latent, here))
        return carry

    lax.fori_loop(0, blocks, one, 0, unroll=8)


def up_grads(place, upq, xs, gp, flat, blat, out, normed):
    blocks = xs.shape[2] // TILE
    xf, scaling = normalised(xs)
    normed[...] = (xf * scaling).astype(BF16)
    up_latent, grad_up_latent = latent(flat, 0), latent(blat, 0)

    def one(p, carry):
        where = place_of(place, p, UP)
        n = column(normed, p)
        there = lanes([of_hidden(gp, upq[PER_ROW * p + i]) for i in range(PER_ROW)])
        product = mm_tn(n, there)
        for i in range(PER_ROW):
            out[(*where, slice(i * TILE, (i + 1) * TILE), slice(None))] = product[
                :, i * TILE : (i + 1) * TILE
            ].astype(BF16)
        out[(*where, slice(MODEL, HIDDEN), slice(None))] = mm_tn(grad_up_latent, n).astype(BF16)
        here = lanes([of_hidden(gp, PER_ROW * p + i) for i in range(PER_ROW)])
        put_low(out, where, mm_tn(up_latent, here))
        return carry

    lax.fori_loop(0, blocks, one, 0, unroll=8)


def grads_kernel(keep, place, upq, dnq, xs, gs, act, gp, flat, blat, out, normed):
    core = place[2]

    @pl.when(core == (UP if keep else DOWN))
    def _():
        up_grads(place, upq, xs, gp, flat, blat, out, normed)

    @pl.when(core == (DOWN if keep else UP))
    def _():
        down_grads(place, dnq, gs, act, flat, blat, out)


def pack_kernel(
    place, up_blocks, up_left, up_right, down_blocks, down_left, down_right, inputs, cotangent,
    mine, other, near_inputs, near_cotangent, sem,
):
    def copies(up, down):
        pairs = [(inputs, near_inputs), (cotangent, near_cotangent)]
        for out, tiles, model, hidden in (
            (up, up_blocks, up_left, up_right),
            (down, down_blocks, down_right, down_left),
        ):
            pairs.append((model, out.at[MODEL:HIDDEN, :]))
            for i in range(PER_ROW):
                rows = slice(HIDDEN + RANK * i, HIDDEN + RANK * (i + 1))
                cols = slice(i * TILE, (i + 1) * TILE)
                pairs.append((tiles.at[i], out.at[cols, :]))
                pairs.append((hidden.at[:, cols], out.at[rows, :]))
        made = [pltpu.make_async_copy(*pair, sem.at[i]) for i, pair in enumerate(pairs)]
        for copy in made[2:] + made[:2]:
            copy.start()
        for copy in made:
            copy.wait()

    @pl.when(place[2] == UP)
    def _():
        copies(mine, other)

    @pl.when(place[2] == DOWN)
    def _():
        copies(other, mine)


def stack_kernel(*refs):
    for d, piece in enumerate(refs[:-1]):
        refs[-1][d] = piece[...]


def spread_kernel(place, *refs):
    mine, other, sides = refs[:ALONG], refs[ALONG : 2 * ALONG], refs[2 * ALONG :]
    z, y, core = place[0], place[1], place[2]
    for side, out in zip((UP, DOWN), sides):
        long_z = far_along_z(place, side)
        for pieces, holder in ((mine, side), (other, 1 - side)):

            @pl.when(core == holder)
            def _():
                for outer in range(ALONG):
                    for inner in range(ALONG):
                        dz = jnp.where(long_z, outer, inner)
                        dy = outer + inner - dz
                        back_z = lax.rem(z - dz + ALONG, ALONG)
                        back_y = lax.rem(y - dy + ALONG, ALONG)
                        chip = back_z * ALONG + back_y
                        for far in range(CORES):
                            out[chip * CORES + (side + far) % CORES] = pieces[outer][inner, far]


def add_cores_kernel(mine, came, *outs):
    for outer, out in enumerate(outs):
        for inner in range(ALONG):
            total = mine[outer, inner].astype(F32) + came[outer, inner].astype(F32)
            out[inner] = total.astype(BF16)


def add_far_kernel(*refs):
    terms, outs = refs[:ALONG], refs[ALONG:]
    for inner, out in enumerate(outs):
        total = terms[0][inner].astype(F32)
        for came in terms[1:]:
            total += came[inner].astype(F32)
        out[...] = total.astype(BF16)


def add_last_kernel(*refs):
    terms, outs = refs[:ALONG], refs[ALONG:]
    for far, out in enumerate(outs):
        total = terms[0][far].astype(F32)
        for came in terms[1:]:
            total += came[far].astype(F32)
        out[...] = total


def finish_kernel(place, mine, other, *outs):
    for side, (tiles, model, hidden) in ((UP, outs[:3]), (DOWN, outs[3:])):
        for total, core in ((mine, side), (other, 1 - side)):

            @pl.when(place[2] == core)
            def _():
                for i in range(PER_ROW):
                    tiles[i] = total[i * TILE : (i + 1) * TILE, :]
                model[...] = total[MODEL:HIDDEN, :]
                for i in range(PER_ROW):
                    rows = slice(HIDDEN + RANK * i, HIDDEN + RANK * (i + 1))
                    hidden[:, i * TILE : (i + 1) * TILE] = total[rows, :]


SMEM = pl.BlockSpec(memory_space=pltpu.SMEM)
VMEM = pl.BlockSpec(memory_space=pltpu.VMEM)
HBM = pl.BlockSpec(memory_space=pl.ANY)


def near(array):
    return pltpu.with_memory_space_constraint(array, pltpu.VMEM)


def forward_call(moment, place, upq, dnq, inputs, incoming, packed, kept):
    rows, width = incoming.shape
    hidden = packed[0].shape[0] * PER_ROW
    return pl.pallas_call(
        partial(forward_kernel, moment),
        out_shape=(pltpu.VMEM(incoming.shape, BF16),)
        + tuple(pltpu.VMEM(item.shape, item.dtype) for item in kept),
        in_specs=[SMEM] * 3 + [VMEM] * (4 + len(kept)),
        out_specs=(VMEM,) * (1 + len(kept)),
        input_output_aliases={7 + i: 1 + i for i in range(len(kept))},
        scratch_shapes=[
            pltpu.VMEM((hidden, rows, TILE), F32),
            pltpu.VMEM((hidden // PER_ROW, rows, TILE), BF16),
        ],
        compiler_params=pltpu.CompilerParams(vmem_limit_bytes=LAYER_VMEM),
        cost_estimate=pl.CostEstimate(flops=10**9, bytes_accessed=10**7, transcendentals=0),
        name="layer_forward",
    )(place, upq, dnq, *map(near, (inputs, incoming, *packed, *kept)))


def backward_call(moment, sections, place, upq, dnq, cotangent, incoming, packed, xs, kept):
    rows, width = incoming.shape
    hidden = packed[0].shape[0] * PER_ROW
    return pl.pallas_call(
        partial(backward_kernel, moment, sections),
        out_shape=(pltpu.VMEM(incoming.shape, BF16),)
        + tuple(pltpu.VMEM(item.shape, item.dtype) for item in kept),
        in_specs=[SMEM] * 3 + [VMEM] * (5 + len(kept)),
        out_specs=(VMEM,) * (1 + len(kept)),
        input_output_aliases={8 + i: 1 + i for i in range(len(kept))},
        scratch_shapes=[
            pltpu.VMEM((hidden, rows, TILE), F32),
            pltpu.VMEM((rows, width), F32),
            pltpu.VMEM((rows, width), F32),
        ],
        compiler_params=pltpu.CompilerParams(vmem_limit_bytes=LAYER_VMEM),
        cost_estimate=pl.CostEstimate(flops=10**9, bytes_accessed=10**7, transcendentals=0),
        name="layer_backward",
    )(place, upq, dnq, *map(near, (cotangent, incoming, *packed, xs, *kept)))


def near_call(kernel, name, shapes, scalars, arrays, scratch=(), far=False):
    specs = [SMEM] * len(scalars) + [VMEM] * len(arrays)
    made = jax.ShapeDtypeStruct if far else pltpu.VMEM
    return pl.pallas_call(
        kernel,
        out_shape=tuple(made(*shape) for shape in shapes),
        in_specs=specs,
        out_specs=(VMEM,) * len(shapes),
        scratch_shapes=list(scratch),
        compiler_params=pltpu.CompilerParams(vmem_limit_bytes=SMALL_VMEM),
        name=name,
    )(*scalars, *map(near, arrays))


def send(value, step):
    sections = lax.axis_size("section")

    def index(section, z, y, c):
        return ((section * ALONG + z % ALONG) * ALONG + y % ALONG) * CORES + c % CORES

    route = []
    for section in range(sections):
        for z in range(ALONG):
            for y in range(ALONG):
                for c in range(CORES):
                    dz, dy, dc = step(section, c)
                    target = index(section, z + dz, y + dy, c + dc)
                    route.append((index(section, z, y, c), target))
    return lax.ppermute(value, ("section", "dp"), route)


def swap_cores(value):
    return send(value, lambda section, core: (0, 0, 1))


def along_first(value, d):
    return send(
        value,
        lambda section, core: (0, d, 0) if core == UP and section < Z_SECTIONS else (d, 0, 0),
    )


def along_second(value, d):
    return send(
        value,
        lambda section, core: (d, 0, 0) if core == UP and section < Z_SECTIONS else (0, d, 0),
    )


FAR = range(1, ALONG)


def gather(place, mine, other):
    side = mine.shape
    pair = near_call(
        stack_kernel, "pair", [((CORES, *side), BF16)], (), (mine, swap_cores(other))
    )[0]
    pairs = [pair] + [along_first(pair, d) for d in FAR]
    line = near_call(stack_kernel, "line", [((ALONG, CORES, *side), BF16)], (), pairs)[0]
    lines = [line] + [along_second(line, d) for d in FAR]
    others = [swap_cores(piece) for piece in lines]
    full = ((CORES * ALONG * ALONG, *side), BF16)
    return near_call(spread_kernel, "spread", (full, full), (place,), lines + others)


def scatter_sum(place, keep, give):
    side = keep.shape[3:]
    line, pair = ((ALONG, CORES, *side), BF16), ((CORES, *side), BF16)
    came = swap_cores(give)
    lines = near_call(add_cores_kernel, "add_cores", [line] * ALONG, (), (keep, came))
    terms = [lines[0]] + [along_second(lines[d], d) for d in FAR]
    pairs = near_call(add_far_kernel, "add_far", [pair] * ALONG, (), terms)
    terms = [pairs[0]] + [along_first(pairs[d], d) for d in FAR]
    mine, other = near_call(add_last_kernel, "add_last", [(side, F32)] * CORES, (), terms)
    three = (((PER_ROW, TILE, TILE), F32), ((RANK, TILE), F32), ((RANK, MODEL), F32))
    return near_call(
        finish_kernel, "finish", three + three, (place,), (mine, swap_cores(other)), far=True
    )


def buffers(after, *shapes):
    shapes = [(shape, BF16) for shape in shapes]
    return near_call(lambda *refs: None, "buffers", shapes, (), (after,))


def hops(moment, micro, sections, backward):
    first = moment // MOMENT_GROUP * MOMENT_GROUP
    steps = [
        step
        for step in range(sections - 1)
        if any(0 <= first + i - 2 * step < micro for i in range(MOMENT_GROUP))
    ]
    if backward:
        return [(sections - 1 - step, sections - 2 - step) for step in steps]
    return [(step, step + 1) for step in steps]


def per_device(
    inputs, cotangent, up_blocks, up_index, up_left, up_right, down_blocks, down_index,
    down_left, down_right,
):
    sections = lax.axis_size("section")
    micro, rows, width = inputs.shape
    hidden = width // TILE * PER_ROW
    rank = lax.axis_index("dp")
    place = jnp.stack(
        [
            rank // (ALONG * CORES),
            rank // CORES % ALONG,
            rank % CORES,
            lax.axis_index("section"),
        ]
    ).astype(jnp.int32)
    place, upq, dnq = lax.optimization_barrier((place, up_index[0, :, 1], down_index[0, :, 0]))
    side = ((SIDE, TILE), BF16)
    factors = [item[0].T for item in (up_left, up_right, down_left, down_right)]
    near_tokens = (inputs.shape, BF16)
    mine, other, inputs, cotangent = pl.pallas_call(
        pack_kernel,
        out_shape=tuple(pltpu.VMEM(*shape) for shape in (side, side, near_tokens, near_tokens)),
        in_specs=[SMEM] + [HBM] * 8,
        out_specs=(VMEM,) * 4,
        scratch_shapes=[pltpu.SemaphoreType.DMA((2 + 2 * (1 + 2 * PER_ROW),))],
        compiler_params=pltpu.CompilerParams(vmem_limit_bytes=SMALL_VMEM),
        name="pack",
    )(
        place,
        *(
            pltpu.with_memory_space_constraint(item, pltpu.HBM)
            for item in (
                up_blocks[0], *factors[:2], down_blocks[0], *factors[2:], inputs, cotangent
            )
        ),
    )
    packed = gather(place, mine, other)

    wide, tall, thin = (micro, rows, width), (micro, hidden, rows, TILE), (micro, 2, rows, TILE)
    xs, outs, act, slope, flat, arrived, travelling = buffers(
        packed[0], wide, wide, tall, tall, thin, (rows, width), (rows, width)
    )
    moments = micro + 2 * (sections - 1)
    for moment in range(moments):
        result, xs, outs, act, slope, flat = forward_call(
            moment, place, upq, dnq, inputs, arrived, packed, (xs, outs, act, slope, flat)
        )
        arrived = travelling
        if moment < moments - 2:
            travelling = lax.ppermute(result, "section", hops(moment, micro, sections, False))

    gs, blat, arrived, travelling = buffers(act, wide, thin, (rows, width), (rows, width))
    gp = slope
    for moment in range(moments):
        result, gs, gp, blat = backward_call(
            moment, sections, place, upq, dnq, cotangent, arrived, packed, xs, (gs, gp, blat)
        )
        arrived = travelling
        if moment < moments - 2:
            travelling = lax.ppermute(result, "section", hops(moment, micro, sections, True))

    terms = [
        near_call(
            partial(grads_kernel, keep),
            "grads",
            [((ALONG, ALONG, CORES, SIDE, TILE), BF16)],
            (place, upq, dnq),
            (xs, gs, act, gp, flat, blat),
            (pltpu.VMEM(wide, BF16),),
        )[0]
        for keep in (False, True)
    ]
    up_grad, up_left_grad, up_right_grad, down_grad, down_right_grad, down_left_grad = scatter_sum(
        place, terms[1], terms[0]
    )
    return (
        outs[None],
        up_grad[None],
        up_left_grad.T[None],
        up_right_grad.T[None],
        down_grad[None],
        down_left_grad.T[None],
        down_right_grad.T[None],
    )


def solution(mesh):
    in_specs = (
        P(None, "dp", None),
        P(None, "dp", None),
        P("section", "dp", None, None),
        P("section", None, None),
        P("section", "dp", None),
        P("section", "dp", None),
        P("section", "dp", None, None),
        P("section", None, None),
        P("section", "dp", None),
        P("section", "dp", None),
    )
    out_specs = (
        P("section", None, "dp", None),
        P("section", "dp", None, None),
        P("section", "dp", None),
        P("section", "dp", None),
        P("section", "dp", None, None),
        P("section", "dp", None),
        P("section", "dp", None),
    )
    return jax.shard_map(
        per_device, mesh=mesh, in_specs=in_specs, out_specs=out_specs, check_vma=False
    )
```

```python
import math
from functools import partial

import jax
import jax.numpy as jnp
from jax import lax
from jax.experimental import pallas as pl
from jax.experimental.pallas import tpu as pltpu
from jax.sharding import Mesh
from jax.sharding import PartitionSpec as P

NORM_EPS = 1e-05
GELU_CUBIC = 0.044715
GELU_ROOT = math.sqrt(2.0 / math.pi)

TILE = 128
PER_ROW = 4
RANK = 16
MODEL = PER_ROW * TILE
HIDDEN = MODEL + RANK
SIDE = HIDDEN + PER_ROW * RANK
UP = 0
DOWN = 1
ALONG = 4
CORES = 2
Z_SECTIONS = 4
SMALL_VMEM = 12 * 1024 * 1024
UNROLL = 16
BACKWARD_UNROLL = 32
MOMENT_GROUP = 4
LAYER_VMEM = 12 * 1024 * 1024
F32 = jnp.float32
BF16 = jnp.bfloat16


def mm(left, right):
    return lax.dot_general(left, right, (((1,), (0,)), ((), ())), preferred_element_type=F32)


def mm_nt(left, right):
    return lax.dot_general(left, right, (((1,), (1,)), ((), ())), preferred_element_type=F32)


def mm_tn(left, right):
    return lax.dot_general(left, right, (((0,), (0,)), ((), ())), preferred_element_type=F32)


def lanes(pieces):
    return jnp.concatenate(pieces, axis=1)


def low_rows(side, index):
    return lanes(
        [side[index, HIDDEN + RANK * i : HIDDEN + RANK * (i + 1), :] for i in range(PER_ROW)]
    )


def normalised(x_ref):
    xf = x_ref[...].astype(F32)
    scaling = lax.rsqrt(jnp.mean(xf * xf, axis=-1, keepdims=True) + NORM_EPS)
    return xf, scaling


def slot_at(number, micro):
    live = (number >= 0) & (number < micro)
    return live, jnp.clip(number, 0, micro - 1)


def forward_kernel(
    moment, place, upq, dnq, inputs, incoming, wu, wd, xs_in, outs_in, act_in, slope_in, lat_in,
    y, xs, outs, act, slope, lat,
    pre, nv,
):
    position = place[3]
    live, slot = slot_at(moment - 2 * position, inputs.shape[0])
    blocks = wu.shape[0]
    hidden = pre.shape[0]
    rows = y.shape[0]

    @pl.when(live)
    def _():
        @pl.when(position == 0)
        def _():
            xs[slot] = inputs[slot]

        @pl.when(position != 0)
        def _():
            xs[slot] = incoming[...]

        xf, scaling = normalised(xs.at[slot])
        normed = (xf * scaling).astype(BF16)
        for p in range(blocks):
            nv[p] = normed[:, p * TILE : (p + 1) * TILE]

        def to_latent(j, total):
            pair = lanes([nv[2 * j], nv[2 * j + 1]])
            factor = lanes([wu[2 * j + i, MODEL:HIDDEN, :] for i in range(2)])
            return total + mm_nt(pair, factor)

        none = jnp.zeros((rows, RANK), F32)
        up_latent = lax.fori_loop(0, blocks // 2, to_latent, none, unroll=UNROLL // 2).astype(BF16)
        lat[slot, 0, :, 0:RANK] = up_latent

        def low_rank(p, carry):
            low = mm(up_latent, low_rows(wu, p))
            for i in range(PER_ROW):
                pre[PER_ROW * p + i] = low[:, i * TILE : (i + 1) * TILE]
            return carry

        lax.fori_loop(0, blocks, low_rank, 0, unroll=UNROLL)

        def up_blocks(p, carry):
            product = mm(nv[p], lanes([wu[p, i * TILE : (i + 1) * TILE, :] for i in range(PER_ROW)]))
            where = [upq[PER_ROW * p + i] for i in range(PER_ROW)]
            sums = [pre[q] + product[:, i * TILE : (i + 1) * TILE] for i, q in enumerate(where)]
            for q, value in zip(where, sums):
                pre[q] = value
            return carry

        lax.fori_loop(0, blocks, up_blocks, 0, unroll=UNROLL)

        def gelu(q, carry):
            u = pre[q]
            square = u * u
            bend = jnp.tanh(u * (GELU_ROOT + GELU_ROOT * GELU_CUBIC * square))
            half = 0.5 + 0.5 * bend
            act[slot, q] = (u * half).astype(BF16)
            inner = 0.5 * GELU_ROOT + 1.5 * GELU_ROOT * GELU_CUBIC * square
            slopes = half + (u * inner) * (1.0 - bend * bend)
            slope[slot, q] = slopes.astype(BF16)
            return carry

        lax.fori_loop(0, hidden, gelu, 0, unroll=8)

        def from_hidden(p, total):
            return total + mm_nt(
                lanes([act[slot, PER_ROW * p + i] for i in range(PER_ROW)]), low_rows(wd, p)
            )

        down_latent = lax.fori_loop(0, blocks, from_hidden, none, unroll=UNROLL).astype(BF16)
        lat[slot, 1, :, 0:RANK] = down_latent

        def down_blocks(p, carry):
            left = lanes([act[slot, dnq[PER_ROW * p + i]] for i in range(PER_ROW)])
            product = mm(left, wd[p, 0:MODEL, :])
            product += mm(down_latent, wd[p, MODEL:HIDDEN, :])
            cols = pl.ds(pl.multiple_of(p * TILE, TILE), TILE)
            result = (xs[slot, :, cols].astype(F32) + product).astype(BF16)
            y[:, cols] = result
            outs[slot, :, cols] = result
            return carry

        lax.fori_loop(0, blocks, down_blocks, 0, unroll=UNROLL)


def backward_kernel(
    moment, sections, place, upq, dnq, cotangent, incoming, wu, wd, xs, gs_in, slope, lat_in,
    y, gs, gp, lat,
    ga, norm, unit,
):
    position = place[3]
    live, slot = slot_at(moment - 2 * (sections - 1 - position), cotangent.shape[0])
    blocks = wu.shape[0]
    hidden = ga.shape[0]
    rows = y.shape[0]

    @pl.when(live)
    def _():
        @pl.when(position == sections - 1)
        def _():
            gs[slot] = cotangent[slot]

        @pl.when(position != sections - 1)
        def _():
            gs[slot] = incoming[...]

        def columns(p, count=1):
            return pl.ds(pl.multiple_of(p * TILE, TILE), count * TILE)

        def to_latent(j, total):
            factor = lanes([wd[2 * j + i, MODEL:HIDDEN, :] for i in range(2)])
            return total + mm_nt(gs[slot, :, columns(2 * j, 2)], factor)

        none = jnp.zeros((rows, RANK), F32)
        down = lax.fori_loop(0, blocks // 2, to_latent, none, unroll=BACKWARD_UNROLL // 2).astype(BF16)
        lat[slot, 1, :, 0:RANK] = down

        def low_rank(p, carry):
            low = mm(down, low_rows(wd, p))
            for i in range(PER_ROW):
                ga[PER_ROW * p + i] = low[:, i * TILE : (i + 1) * TILE]
            return carry

        lax.fori_loop(0, blocks, low_rank, 0, unroll=BACKWARD_UNROLL)

        def down_blocks(p, carry):
            product = mm_nt(gs[slot, :, columns(p)], wd[p, 0:MODEL, :])
            where = [dnq[PER_ROW * p + i] for i in range(PER_ROW)]
            sums = [ga[q] + product[:, i * TILE : (i + 1) * TILE] for i, q in enumerate(where)]
            for q, value in zip(where, sums):
                ga[q] = value
            return carry

        lax.fori_loop(0, blocks, down_blocks, 0, unroll=BACKWARD_UNROLL)

        def slopes(q, carry):
            gp[slot, q] = (ga[q] * slope[slot, q].astype(F32)).astype(BF16)
            return carry

        lax.fori_loop(0, hidden, slopes, 0, unroll=8)

        def from_hidden(p, total):
            return total + mm_nt(
                lanes([gp[slot, PER_ROW * p + i] for i in range(PER_ROW)]), low_rows(wu, p)
            )

        up = lax.fori_loop(0, blocks, from_hidden, none, unroll=BACKWARD_UNROLL).astype(BF16)
        lat[slot, 0, :, 0:RANK] = up
        xf, scaling = normalised(xs.at[slot])
        unit[...] = xf * scaling

        def up_blocks(p, along):
            left = lanes([gp[slot, upq[PER_ROW * p + i]] for i in range(PER_ROW)])
            piece = lanes([wu[p, i * TILE : (i + 1) * TILE, :] for i in range(PER_ROW)])
            product = mm_nt(left, piece)
            product += mm(up, wu[p, MODEL:HIDDEN, :])
            norm[:, columns(p)] = product
            return along + product * unit[:, columns(p)]

        along = jnp.zeros((rows, TILE), F32)
        along = lax.fori_loop(0, blocks, up_blocks, along, unroll=BACKWARD_UNROLL)
        mean = jnp.sum(along, axis=-1, keepdims=True) * (1.0 / (blocks * TILE))
        y[...] = (
            gs[slot].astype(F32) + scaling * (norm[...] - unit[...] * mean)
        ).astype(BF16)


def far_along_z(place, side):
    return jnp.logical_and(side == UP, place[3] < Z_SECTIONS)


def place_of(place, p, side):
    dz = lax.rem(p // (ALONG * CORES) - place[0] + ALONG, ALONG)
    dy = lax.rem(lax.rem(p // CORES, ALONG) - place[1] + ALONG, ALONG)
    other = lax.rem(lax.rem(p, CORES) + side, CORES)
    long_z = far_along_z(place, side)
    return jnp.where(long_z, dz, dy), jnp.where(long_z, dy, dz), other


def column(ref, p):
    tokens = ref.shape[0] * ref.shape[1]
    return ref[:, :, pl.ds(pl.multiple_of(p * TILE, TILE), TILE)].reshape(tokens, TILE)


def of_hidden(ref, q):
    return ref[:, pl.ds(q, 1)].reshape(ref.shape[0] * ref.shape[2], TILE)


def latent(ref, kind):
    return ref[:, kind, :, 0:RANK].reshape(ref.shape[0] * ref.shape[2], RANK)


def put_low(out, where, low):
    for i in range(PER_ROW):
        rows = slice(HIDDEN + RANK * i, HIDDEN + RANK * (i + 1))
        out[(*where, rows, slice(None))] = low[:, i * TILE : (i + 1) * TILE].astype(BF16)


def down_grads(place, dnq, gs, act, flat, blat, out):
    blocks = gs.shape[2] // TILE
    down_latent, grad_down_latent = latent(flat, 1), latent(blat, 1)

    def one(p, carry):
        where = place_of(place, p, DOWN)
        g = column(gs, p)
        for i in range(PER_ROW):
            product = mm_tn(of_hidden(act, dnq[PER_ROW * p + i]), g)
            out[(*where, slice(i * TILE, (i + 1) * TILE), slice(None))] = product.astype(BF16)
        out[(*where, slice(MODEL, HIDDEN), slice(None))] = mm_tn(down_latent, g).astype(BF16)
        here = lanes([of_hidden(act, PER_ROW * p + i) for i in range(PER_ROW)])
        put_low(out, where, mm_tn(grad_down_latent, here))
        return carry

    lax.fori_loop(0, blocks, one, 0, unroll=8)


def up_grads(place, upq, xs, gp, flat, blat, out, normed):
    blocks = xs.shape[2] // TILE
    xf, scaling = normalised(xs)
    normed[...] = (xf * scaling).astype(BF16)
    up_latent, grad_up_latent = latent(flat, 0), latent(blat, 0)

    def one(p, carry):
        where = place_of(place, p, UP)
        n = column(normed, p)
        there = lanes([of_hidden(gp, upq[PER_ROW * p + i]) for i in range(PER_ROW)])
        product = mm_tn(n, there)
        for i in range(PER_ROW):
            out[(*where, slice(i * TILE, (i + 1) * TILE), slice(None))] = product[
                :, i * TILE : (i + 1) * TILE
            ].astype(BF16)
        out[(*where, slice(MODEL, HIDDEN), slice(None))] = mm_tn(grad_up_latent, n).astype(BF16)
        here = lanes([of_hidden(gp, PER_ROW * p + i) for i in range(PER_ROW)])
        put_low(out, where, mm_tn(up_latent, here))
        return carry

    lax.fori_loop(0, blocks, one, 0, unroll=8)


def grads_kernel(keep, place, upq, dnq, xs, gs, act, gp, flat, blat, out, normed):
    core = place[2]

    @pl.when(core == (UP if keep else DOWN))
    def _():
        up_grads(place, upq, xs, gp, flat, blat, out, normed)

    @pl.when(core == (DOWN if keep else UP))
    def _():
        down_grads(place, dnq, gs, act, flat, blat, out)


def pack_kernel(
    place, up_blocks, up_left, up_right, down_blocks, down_left, down_right, inputs, cotangent,
    mine, other, near_inputs, near_cotangent, sem,
):
    def copies(up, down):
        pairs = [(inputs, near_inputs), (cotangent, near_cotangent)]
        for out, tiles, model, hidden in (
            (up, up_blocks, up_left, up_right),
            (down, down_blocks, down_right, down_left),
        ):
            pairs.append((model, out.at[MODEL:HIDDEN, :]))
            for i in range(PER_ROW):
                rows = slice(HIDDEN + RANK * i, HIDDEN + RANK * (i + 1))
                cols = slice(i * TILE, (i + 1) * TILE)
                pairs.append((tiles.at[i], out.at[cols, :]))
                pairs.append((hidden.at[:, cols], out.at[rows, :]))
        made = [pltpu.make_async_copy(*pair, sem.at[i]) for i, pair in enumerate(pairs)]
        for copy in made[2:] + made[:2]:
            copy.start()
        for copy in made:
            copy.wait()

    @pl.when(place[2] == UP)
    def _():
        copies(mine, other)

    @pl.when(place[2] == DOWN)
    def _():
        copies(other, mine)


def stack_kernel(*refs):
    for d, piece in enumerate(refs[:-1]):
        refs[-1][d] = piece[...]


def spread_kernel(place, *refs):
    mine, other, sides = refs[:ALONG], refs[ALONG : 2 * ALONG], refs[2 * ALONG :]
    z, y, core = place[0], place[1], place[2]
    for side, out in zip((UP, DOWN), sides):
        long_z = far_along_z(place, side)
        for pieces, holder in ((mine, side), (other, 1 - side)):

            @pl.when(core == holder)
            def _():
                for outer in range(ALONG):
                    for inner in range(ALONG):
                        dz = jnp.where(long_z, outer, inner)
                        dy = outer + inner - dz
                        back_z = lax.rem(z - dz + ALONG, ALONG)
                        back_y = lax.rem(y - dy + ALONG, ALONG)
                        chip = back_z * ALONG + back_y
                        for far in range(CORES):
                            out[chip * CORES + (side + far) % CORES] = pieces[outer][inner, far]


def add_cores_kernel(mine, came, *outs):
    for outer, out in enumerate(outs):
        for inner in range(ALONG):
            total = mine[outer, inner].astype(F32) + came[outer, inner].astype(F32)
            out[inner] = total.astype(BF16)


def add_far_kernel(*refs):
    terms, outs = refs[:ALONG], refs[ALONG:]
    for inner, out in enumerate(outs):
        total = terms[0][inner].astype(F32)
        for came in terms[1:]:
            total += came[inner].astype(F32)
        out[...] = total.astype(BF16)


def add_last_kernel(*refs):
    terms, outs = refs[:ALONG], refs[ALONG:]
    for far, out in enumerate(outs):
        total = terms[0][far].astype(F32)
        for came in terms[1:]:
            total += came[far].astype(F32)
        out[...] = total


def finish_kernel(place, mine, other, *outs):
    for side, (tiles, model, hidden) in ((UP, outs[:3]), (DOWN, outs[3:])):
        for total, core in ((mine, side), (other, 1 - side)):

            @pl.when(place[2] == core)
            def _():
                for i in range(PER_ROW):
                    tiles[i] = total[i * TILE : (i + 1) * TILE, :]
                model[...] = total[MODEL:HIDDEN, :]
                for i in range(PER_ROW):
                    rows = slice(HIDDEN + RANK * i, HIDDEN + RANK * (i + 1))
                    hidden[:, i * TILE : (i + 1) * TILE] = total[rows, :]


SMEM = pl.BlockSpec(memory_space=pltpu.SMEM)
VMEM = pl.BlockSpec(memory_space=pltpu.VMEM)
HBM = pl.BlockSpec(memory_space=pl.ANY)


def near(array):
    return pltpu.with_memory_space_constraint(array, pltpu.VMEM)


def forward_call(moment, place, upq, dnq, inputs, incoming, packed, kept):
    rows, width = incoming.shape
    hidden = packed[0].shape[0] * PER_ROW
    return pl.pallas_call(
        partial(forward_kernel, moment),
        out_shape=(pltpu.VMEM(incoming.shape, BF16),)
        + tuple(pltpu.VMEM(item.shape, item.dtype) for item in kept),
        in_specs=[SMEM] * 3 + [VMEM] * (4 + len(kept)),
        out_specs=(VMEM,) * (1 + len(kept)),
        input_output_aliases={7 + i: 1 + i for i in range(len(kept))},
        scratch_shapes=[
            pltpu.VMEM((hidden, rows, TILE), F32),
            pltpu.VMEM((hidden // PER_ROW, rows, TILE), BF16),
        ],
        compiler_params=pltpu.CompilerParams(vmem_limit_bytes=LAYER_VMEM),
        cost_estimate=pl.CostEstimate(flops=10**9, bytes_accessed=10**7, transcendentals=0),
        name="layer_forward",
    )(place, upq, dnq, *map(near, (inputs, incoming, *packed, *kept)))


def backward_call(moment, sections, place, upq, dnq, cotangent, incoming, packed, xs, kept):
    rows, width = incoming.shape
    hidden = packed[0].shape[0] * PER_ROW
    return pl.pallas_call(
        partial(backward_kernel, moment, sections),
        out_shape=(pltpu.VMEM(incoming.shape, BF16),)
        + tuple(pltpu.VMEM(item.shape, item.dtype) for item in kept),
        in_specs=[SMEM] * 3 + [VMEM] * (5 + len(kept)),
        out_specs=(VMEM,) * (1 + len(kept)),
        input_output_aliases={8 + i: 1 + i for i in range(len(kept))},
        scratch_shapes=[
            pltpu.VMEM((hidden, rows, TILE), F32),
            pltpu.VMEM((rows, width), F32),
            pltpu.VMEM((rows, width), F32),
        ],
        compiler_params=pltpu.CompilerParams(vmem_limit_bytes=LAYER_VMEM),
        cost_estimate=pl.CostEstimate(flops=10**9, bytes_accessed=10**7, transcendentals=0),
        name="layer_backward",
    )(place, upq, dnq, *map(near, (cotangent, incoming, *packed, xs, *kept)))


def near_call(kernel, name, shapes, scalars, arrays, scratch=(), far=False):
    specs = [SMEM] * len(scalars) + [VMEM] * len(arrays)
    made = jax.ShapeDtypeStruct if far else pltpu.VMEM
    return pl.pallas_call(
        kernel,
        out_shape=tuple(made(*shape) for shape in shapes),
        in_specs=specs,
        out_specs=(VMEM,) * len(shapes),
        scratch_shapes=list(scratch),
        compiler_params=pltpu.CompilerParams(vmem_limit_bytes=SMALL_VMEM),
        name=name,
    )(*scalars, *map(near, arrays))


def send(value, step):
    sections = lax.axis_size("section")

    def index(section, z, y, c):
        return ((section * ALONG + z % ALONG) * ALONG + y % ALONG) * CORES + c % CORES

    route = []
    for section in range(sections):
        for z in range(ALONG):
            for y in range(ALONG):
                for c in range(CORES):
                    dz, dy, dc = step(section, c)
                    target = index(section, z + dz, y + dy, c + dc)
                    route.append((index(section, z, y, c), target))
    return lax.ppermute(value, ("section", "dp"), route)


def swap_cores(value):
    return send(value, lambda section, core: (0, 0, 1))


def along_first(value, d):
    return send(
        value,
        lambda section, core: (0, d, 0) if core == UP and section < Z_SECTIONS else (d, 0, 0),
    )


def along_second(value, d):
    return send(
        value,
        lambda section, core: (d, 0, 0) if core == UP and section < Z_SECTIONS else (0, d, 0),
    )


FAR = range(1, ALONG)


def gather(place, mine, other):
    side = mine.shape
    pair = near_call(
        stack_kernel, "pair", [((CORES, *side), BF16)], (), (mine, swap_cores(other))
    )[0]
    pairs = [pair] + [along_first(pair, d) for d in FAR]
    line = near_call(stack_kernel, "line", [((ALONG, CORES, *side), BF16)], (), pairs)[0]
    lines = [line] + [along_second(line, d) for d in FAR]
    others = [swap_cores(piece) for piece in lines]
    full = ((CORES * ALONG * ALONG, *side), BF16)
    return near_call(spread_kernel, "spread", (full, full), (place,), lines + others)


def scatter_sum(place, keep, give):
    side = keep.shape[3:]
    line, pair = ((ALONG, CORES, *side), BF16), ((CORES, *side), BF16)
    came = swap_cores(give)
    lines = near_call(add_cores_kernel, "add_cores", [line] * ALONG, (), (keep, came))
    terms = [lines[0]] + [along_second(lines[d], d) for d in FAR]
    pairs = near_call(add_far_kernel, "add_far", [pair] * ALONG, (), terms)
    terms = [pairs[0]] + [along_first(pairs[d], d) for d in FAR]
    mine, other = near_call(add_last_kernel, "add_last", [(side, F32)] * CORES, (), terms)
    three = (((PER_ROW, TILE, TILE), F32), ((RANK, TILE), F32), ((RANK, MODEL), F32))
    return near_call(
        finish_kernel, "finish", three + three, (place,), (mine, swap_cores(other)), far=True
    )


def buffers(after, *shapes):
    shapes = [(shape, BF16) for shape in shapes]
    return near_call(lambda *refs: None, "buffers", shapes, (), (after,))


def hops(moment, micro, sections, backward):
    first = moment // MOMENT_GROUP * MOMENT_GROUP
    steps = [
        step
        for step in range(sections - 1)
        if any(0 <= first + i - 2 * step < micro for i in range(MOMENT_GROUP))
    ]
    if backward:
        return [(sections - 1 - step, sections - 2 - step) for step in steps]
    return [(step, step + 1) for step in steps]


def per_device(
    inputs, cotangent, up_blocks, up_index, up_left, up_right, down_blocks, down_index,
    down_left, down_right,
):
    sections = lax.axis_size("section")
    micro, rows, width = inputs.shape
    hidden = width // TILE * PER_ROW
    rank = lax.axis_index("dp")
    place = jnp.stack(
        [
            rank // (ALONG * CORES),
            rank // CORES % ALONG,
            rank % CORES,
            lax.axis_index("section"),
        ]
    ).astype(jnp.int32)
    place, upq, dnq = lax.optimization_barrier((place, up_index[0, :, 1], down_index[0, :, 0]))
    side = ((SIDE, TILE), BF16)
    factors = [item[0].T for item in (up_left, up_right, down_left, down_right)]
    near_tokens = (inputs.shape, BF16)
    mine, other, inputs, cotangent = pl.pallas_call(
        pack_kernel,
        out_shape=tuple(pltpu.VMEM(*shape) for shape in (side, side, near_tokens, near_tokens)),
        in_specs=[SMEM] + [HBM] * 8,
        out_specs=(VMEM,) * 4,
        scratch_shapes=[pltpu.SemaphoreType.DMA((2 + 2 * (1 + 2 * PER_ROW),))],
        compiler_params=pltpu.CompilerParams(vmem_limit_bytes=SMALL_VMEM),
        name="pack",
    )(
        place,
        *(
            pltpu.with_memory_space_constraint(item, pltpu.HBM)
            for item in (
                up_blocks[0], *factors[:2], down_blocks[0], *factors[2:], inputs, cotangent
            )
        ),
    )
    packed = gather(place, mine, other)

    wide, tall, thin = (micro, rows, width), (micro, hidden, rows, TILE), (micro, 2, rows, TILE)
    xs, outs, act, slope, flat, arrived, travelling = buffers(
        packed[0], wide, wide, tall, tall, thin, (rows, width), (rows, width)
    )
    moments = micro + 2 * (sections - 1)
    for moment in range(moments):
        result, xs, outs, act, slope, flat = forward_call(
            moment, place, upq, dnq, inputs, arrived, packed, (xs, outs, act, slope, flat)
        )
        arrived = travelling
        if moment < moments - 2:
            travelling = lax.ppermute(result, "section", hops(moment, micro, sections, False))

    gs, blat, arrived, travelling = buffers(act, wide, thin, (rows, width), (rows, width))
    gp = slope
    for moment in range(moments):
        result, gs, gp, blat = backward_call(
            moment, sections, place, upq, dnq, cotangent, arrived, packed, xs, (gs, gp, blat)
        )
        arrived = travelling
        if moment < moments - 2:
            travelling = lax.ppermute(result, "section", hops(moment, micro, sections, True))

    terms = [
        near_call(
            partial(grads_kernel, keep),
            "grads",
            [((ALONG, ALONG, CORES, SIDE, TILE), BF16)],
            (place, upq, dnq),
            (xs, gs, act, gp, flat, blat),
            (pltpu.VMEM(wide, BF16),),
        )[0]
        for keep in (False, True)
    ]
    up_grad, up_left_grad, up_right_grad, down_grad, down_right_grad, down_left_grad = scatter_sum(
        place, terms[1], terms[0]
    )
    return (
        outs[None],
        up_grad[None],
        up_left_grad.T[None],
        up_right_grad.T[None],
        down_grad[None],
        down_left_grad.T[None],
        down_right_grad.T[None],
    )


def solution(mesh):
    in_specs = (
        P(None, "dp", None),
        P(None, "dp", None),
        P("section", "dp", None, None),
        P("section", None, None),
        P("section", "dp", None),
        P("section", "dp", None),
        P("section", "dp", None, None),
        P("section", None, None),
        P("section", "dp", None),
        P("section", "dp", None),
    )
    out_specs = (
        P("section", None, "dp", None),
        P("section", "dp", None, None),
        P("section", "dp", None),
        P("section", "dp", None),
        P("section", "dp", None, None),
        P("section", "dp", None),
        P("section", "dp", None),
    )
    return jax.shard_map(
        per_device, mesh=mesh, in_specs=in_specs, out_specs=out_specs, check_vma=False
    )
```
